128 devices in a mesh: param: 8 (over y, z_hi), obs: 16 (over x, z_lo, core).
Axes of the slice: x: 4, y: 4, z: 4 (z_hi: 2, z_lo: 2; z = z_hi * 2 + z_lo), core: 2. Of those that a mesh axis runs over, the one named last changes fastest.
Arguments:
- design: bfloat16 [10240, 8192], P('obs', 'param'), may hold values from -6 to 6
- observed: bfloat16 [10240], P('obs'), may hold values from -6 to 6
- row_weight: float32 [10240], P('obs'), may hold values from 0.3 to 3
- taps: float32 [7], replicated, may hold values from -0.5 to 0.5
Outputs:
- normal: float32 [8192, 8192], P('obs', 'param')
- rhs: float32 [8192], P('param')
- filtered_obs: float32 [10240], P('obs')
The draws below stay inside these ranges and needn't reach their ends.
All inputs are finite; a program needn't handle non-finite values.
Results may differ from the reference program's by a relative error of at most 0.0035.
Values may be sent and summed in bfloat16 or wider, within the bound.
A program may use at most 128 MiB of HBM per device.

```python
import math
import jax
import jax.numpy as jnp

P_SIZE = 8192
LAGS = 7
ROWS = 10240


def block_levels(own_key, shape, pieces, smallest, largest):
    gain, own = 1.0, jax.random.fold_in(own_key, 6)
    for axis_at, shards_of in pieces:
        heights = jnp.exp(jax.random.uniform(jax.random.fold_in(own, axis_at), (shards_of,), jnp.float32, smallest / len(pieces), largest / len(pieces)))
        gain = gain * jnp.repeat(heights, shape[axis_at] // shards_of).reshape([-1 if axis == axis_at else 1 for axis in range(len(shape))])
    return gain


def gaussian(rng, dims, deviation, limit, split=(), dtype=jnp.bfloat16):
    level = block_levels(rng, dims, split, -0.22, 0.18) if split else 1.0
    result = jax.random.normal(rng, dims, jnp.float32) * deviation * level
    return jnp.minimum(jnp.maximum(result, -limit), limit).astype(dtype)


def setup_inputs(seed: int = 0) -> dict:
    key_list = jax.random.split(jax.random.key(seed), 5)
    return {
        "design": gaussian(key_list[0], (ROWS, P_SIZE), 1.0, 6.0, ((0, 16), (1, 8))),
        "observed": gaussian(key_list[1], (ROWS,), 1.0, 6.0, ((0, 16),)),
        "row_weight": jnp.clip(jnp.exp(math.log(3.0) - 2.3025851 * jax.random.uniform(key_list[2], (ROWS,), jnp.float32) ** block_levels(key_list[2], (ROWS,), ((0, 16),), -0.2, 0.2)), 0.3, 3.0),
        "taps": jnp.clip(jax.random.uniform(key_list[3], (LAGS,), jnp.float32, -0.5, 0.5), -0.5, 0.5),
    }


def apply_filter(values, taps):
    total = values.astype(jnp.float32)
    for lag in range(1, LAGS + 1):
        earlier = jnp.concatenate([jnp.zeros((lag,) + values.shape[1:], jnp.float32), values[:-lag].astype(jnp.float32)], 0)
        total = total + taps[lag - 1] * earlier
    return total

def reference(design, observed, row_weight, taps):
    filtered = apply_filter(design, taps).astype(jnp.bfloat16)
    filtered_obs = apply_filter(observed, taps)
    weighted = (row_weight[:, None] * filtered.astype(jnp.float32)).astype(jnp.bfloat16)
    weighted_obs = (row_weight * filtered_obs).astype(jnp.bfloat16)
    normal = jnp.dot(filtered.T, weighted, preferred_element_type=jnp.float32) / ROWS
    rhs = jnp.dot(weighted_obs, filtered, preferred_element_type=jnp.float32) / math.sqrt(ROWS)
    return (normal, rhs, filtered_obs)
```

```python
import functools
import math

import jax
import jax.numpy as jnp
from jax import lax
from jax.experimental import pallas as pl
from jax.experimental.pallas import tpu as pltpu
from jax.sharding import PartitionSpec as P

MESH = pl.DeviceIdType.MESH
BF16, F32 = jnp.bfloat16, jnp.float32
ROWS = 640
COLS = 1024
LAGS = 7
PART = 256
DEPTH = 2 * ROWS


def kernel(
    scale, rhs_scale,
    design, observed, weight, taps,
    normal, rhs, filtered_obs,
    ext, halo, obs_tail, obs_halo, wcol, sent, weighted, rows, cols, part, own, from_left, from_right, far_left, far_right,
    leaving, landed, rhs_all,
    halo_s, halo_r, rows_s, rows_f, rows_sib, rows_r, cols_s, cols_sib, cols_f, cols_r, x_s, x_r, z_s, z_r, rhs_s, rhs_r,
):
    p, o = lax.axis_index("param"), lax.axis_index("obs")
    y, h = p // 2, p % 2
    x, l, k = o // 4, (o // 2) % 2, o % 2
    near = (y - x + 4) % 4
    settled = l == h

    def param_of(y_, h_):
        return ((y_ + 4) % 4) * 2 + h_

    def obs_of(x_, l_, k_):
        return ((x_ + 4) % 4) * 4 + l_ * 2 + k_

    sibling = (p, obs_of(x, l, 1 - k))
    up = [(param_of(y + 1, h), obs_of(x, l, k)), (param_of(y + 1, h), obs_of(x, l, 1 - k))]
    down = [(param_of(y - 1, h), obs_of(x, l, k)), (param_of(y - 1, h), obs_of(x, l, 1 - k))]
    right, left = (p, obs_of(x + 1, l, k)), (p, obs_of(x - 1, l, k))
    across = (param_of(y, 1 - h), o)
    beside = (p, obs_of(x, 1 - l, k))
    corner = (param_of(y, 1 - h), obs_of(x, 1 - l, k))
    following = (p, (o + 1) % 16)

    def remote(src, dst, send, recv, device):
        return pltpu.make_async_remote_copy(
            src_ref=src, dst_ref=dst, send_sem=send, recv_sem=recv, device_id=device, device_id_type=MESH
        )

    def halo_copies():
        return (
            remote(design.at[pl.ds(ROWS - 16, 16), :], halo, halo_s.at[0], halo_r.at[0], following),
            remote(obs_tail, obs_halo, halo_s.at[1], halo_r.at[1], following),
        )

    def own_piece(m, rel):
        return rows.at[0, m, :, pl.ds(0, ROWS)] if rel == 0 else sent.at[m]

    def lanes(rel):
        return pl.ds(ROWS * rel, ROWS)

    def rows_up(m, rel):
        return remote(own_piece(m, rel), rows.at[3, m, :, lanes(rel)], rows_s.at[0, m, rel], rows_r.at[3, m, rel], up[rel])

    def rows_down(m, rel):
        return remote(own_piece(m, rel), rows.at[1, m, :, lanes(rel)], rows_s.at[1, m, rel], rows_r.at[1, m, rel], down[rel])

    def rows_on(m, rel):
        source = rows.at[3 if m == 0 else 1, m, :, lanes(rel)]
        return remote(
            source, rows.at[2, m, :, lanes(rel)], rows_f.at[m, rel], rows_r.at[2, m, rel], up[0] if m == 0 else down[0]
        )

    def rows_over(m):
        return remote(sent.at[m], rows.at[0, m, :, lanes(1)], rows_sib.at[m], rows_r.at[0, m, 1], sibling)

    def cols_over(n):
        half = pl.ds(0, ROWS)
        return remote(cols.at[0, n, half, :], cols.at[0, n, pl.ds(ROWS, ROWS), :], cols_sib.at[n], cols_r.at[0, n, 1], sibling)

    def cols_across(n):
        half = pl.ds(0, ROWS)
        return remote(cols.at[0, n, half, :], cols.at[1, n, half, :], cols_s.at[n], cols_r.at[1, n, 0], across)

    def cols_on(n):
        half = pl.ds(0, ROWS)
        return remote(cols.at[1, n, half, :], cols.at[1, n, pl.ds(ROWS, ROWS), :], cols_f.at[n], cols_r.at[1, n, 1], sibling)

    def x_far(d, hr):
        dst = (far_left if d == 0 else far_right).at[hr]
        return remote(part.at[1, d, hr], dst, x_s.at[d, 0, hr], x_r.at[d, 0, hr], right if d == 0 else left)

    def x_raw(d, hr):
        m = 1 - d
        dst = (from_left if d == 0 else from_right).at[m, hr]
        return remote(part.at[0 if d == 0 else 2, m, hr], dst, x_s.at[d, 1, hr], x_r.at[d, 1, hr], right if d == 0 else left)

    def x_sum(d, hr):
        m = d
        dst = (from_left if d == 0 else from_right).at[m, hr]
        return remote(part.at[0 if d == 0 else 2, m, hr], dst, x_s.at[d, 2, hr], x_r.at[d, 2, hr], right if d == 0 else left)

    def z_beside(m):
        return remote(leaving.at[0, m], landed.at[0, m], z_s.at[0, m], z_r.at[0, m], beside)

    def z_across(m):
        return remote(leaving.at[1, m], landed.at[0, m], z_s.at[1, m], z_r.at[0, m], across)

    def z_corner(m):
        return remote(leaving.at[1, m], landed.at[1, m], z_s.at[1, m], z_r.at[1, m], corner)

    def rhs_to(step):
        peer = (p, (o + step) % 16)
        return remote(rhs_all.at[o], rhs_all.at[o], rhs_s.at[step], rhs_r.at[step], peer)

    barrier = pltpu.get_barrier_semaphore()
    greeted = up + down + [across, corner] + [(p, (o + step) % 16) for step in range(1, 16)]
    for device in greeted:
        pl.semaphore_signal(barrier, inc=1, device_id=device, device_id_type=MESH)

    signal_row = jnp.broadcast_to(observed[...].astype(F32), (8, ROWS))
    weight_row = jnp.broadcast_to(weight[...], (8, ROWS))
    obs_tail[...] = signal_row[:, ROWS - 128 :]
    for r in range(ROWS // 128):
        block = jnp.broadcast_to(weight[:, r * 128 : (r + 1) * 128], (128, 128))
        wcol[pl.ds(r * 128, 128), :] = block.T

    def widen(i, _):
        at = pl.multiple_of(i * 128, 128)
        ext[pl.ds(8, ROWS), pl.ds(at, 128)] = design[:, pl.ds(at, 128)].astype(F32)
        return 0

    lax.fori_loop(0, COLS // 128, widen, 0)
    pl.semaphore_wait(barrier, len(greeted))

    @pl.when(o < 15)
    def _():
        for copy in halo_copies():
            copy.start()

    @pl.when(o > 0)
    def _():
        for copy in halo_copies():
            copy.wait_recv()
        ext[pl.ds(0, 8), :] = halo[...].astype(F32)[8:]

    @pl.when(o == 0)
    def _():
        ext[pl.ds(0, 8), :] = jnp.zeros((8, COLS), F32)
        obs_halo[...] = jnp.zeros((8, 128), F32)

    def filter_piece(m, rel):
        core = k if rel == 0 else 1 - k

        def block(c, _):
            within = pl.multiple_of(c * 128, 128)
            at = pl.multiple_of(core * 512 + m * PART + within, 128)
            for r in range(ROWS // 128):
                first = r * 128
                total = ext[pl.ds(8 + first, 128), pl.ds(at, 128)]
                for lag in range(1, LAGS + 1):
                    total = total + taps[lag - 1] * ext[pl.ds(8 + first - lag, 128), pl.ds(at, 128)]
                rounded = total.astype(BF16).astype(F32)
                scaled = (wcol[pl.ds(first, 128), :] * rounded).astype(BF16)
                cols[0, core, pl.ds(first, 128), pl.ds(pl.multiple_of(m * PART + within, 128), 128)] = scaled
                turned = rounded.T.astype(BF16)
                if rel == 0:
                    rows[0, m, pl.ds(within, 128), pl.ds(first, 128)] = turned
                else:
                    sent[m, pl.ds(within, 128), pl.ds(first, 128)] = turned
            return 0

        lax.fori_loop(0, PART // 128, block, 0)

    first_far = near == 2
    for m in range(2):
        for rel in (1, 0):
            filter_piece(m, rel)
            (rows_up if m == 0 else rows_down)(m, rel).start()
            if rel == 1:
                rows_over(m).start()
    for n in range(2):
        cols_over(n).start()
        cols_across(n).start()

    @pl.when(first_far)
    def _():
        for rel in (1, 0):
            rows_up(1, rel).start()
            rows_down(0, rel).start()

    extended = jnp.concatenate([obs_halo[...], signal_row], axis=1)
    total = signal_row
    for lag in range(1, LAGS + 1):
        total = total + taps[lag - 1] * pltpu.roll(extended, lag, 1)[:, 128:]
    filtered_obs[...] = total[0:1, :]
    weighted[...] = jnp.concatenate([weight_row * total, weight_row * total], axis=0).astype(BF16)
    line = lax.broadcasted_iota(jnp.int32, (8, 128), 0)
    sums = jnp.zeros((8, 128), F32)
    for m in range(2):
        for rel in range(2):
            core = k if rel == 0 else 1 - k
            piece = rows[0, m, :, pl.ds(0, ROWS)] if rel == 0 else sent[m]
            dots = lax.dot_general(weighted[...], piece, (((1,), (1,)), ((), ())), preferred_element_type=F32)
            for c in range(2):
                sums = jnp.where(line == core * 4 + m * 2 + c, dots[0:8, c * 128 : (c + 1) * 128], sums)
    rhs_all[o] = sums
    for step in range(1, 16):
        rhs_to(step).start()

    def multiply(dy, m, hr):
        role = (near + dy) % 4

        def chunk(c, _):
            at = pl.multiple_of((c % 2) * 256, 256)
            value = jnp.dot(rows[dy, m], cols[hr, c // 2, :, pl.ds(at, 256)], preferred_element_type=F32)
            to = pl.ds(pl.multiple_of(c * 256, 256), 256)

            @pl.when(role == 0)
            def _():
                own[m, hr, :, to] = value

            @pl.when(role != 0)
            def _():
                part[role - 1, m, hr, :, to] = value.astype(BF16)

            return 0

        lax.fori_loop(0, COLS // 256, chunk, 0)

        @pl.when(role == 2)
        def _():
            x_far(m, hr).start()

        @pl.when(role == (1 if m == 1 else 3))
        def _():
            x_raw(1 - m, hr).start()

    for m in range(2):
        rows_over(m).wait_recv()
        cols_over(m).wait_recv()
    for m in range(2):
        multiply(0, m, 0)

    for rel in (1, 0):
        rows_up(0, rel).wait_recv()
        rows_on(0, rel).start()
        rows_down(1, rel).wait_recv()
        rows_on(1, rel).start()

    @pl.when(jnp.logical_not(first_far))
    def _():
        for rel in (1, 0):
            rows_up(1, rel).start()
            rows_down(0, rel).start()

    multiply(3, 0, 0)
    multiply(1, 1, 0)
    for n in range(2):
        cols_across(n).wait_recv()
        cols_on(n).start()
    for n in range(2):
        cols_on(n).wait_recv()
    for m in range(2):
        multiply(0, m, 1)
    multiply(3, 0, 1)
    multiply(1, 1, 1)
    for m in range(2):
        for rel in range(2):
            rows_on(m, rel).wait_recv()
    for hr in range(2):
        for m in range(2):
            multiply(2, m, hr)
    for rel in range(2):
        rows_up(1, rel).wait_recv()
        rows_down(0, rel).wait_recv()
    for hr in range(2):
        multiply(1, 0, hr)
        multiply(3, 1, hr)

    for hr in range(2):
        for d in range(2):
            x_far(d, hr).wait_recv()
            at = 0 if d == 0 else 2
            gained = (far_left if d == 0 else far_right)[hr]
            part[at, d, hr] = (part[at, d, hr].astype(F32) + gained.astype(F32)).astype(BF16)
            x_sum(d, hr).start()

    for step in range(1, 16):
        rhs_to(step).wait_recv()
    total = rhs_all[0]
    for step in range(1, 16):
        total = total + rhs_all[step]
    rhs[...] = total * rhs_scale

    for hr in range(2):
        for m in range(2):
            (x_sum if m == 0 else x_raw)(0, hr).wait_recv()
            (x_sum if m == 1 else x_raw)(1, hr).wait_recv()
            total = own[m, hr] + from_left[m, hr].astype(F32) + from_right[m, hr].astype(F32)
            if hr == 0:

                @pl.when(settled)
                def _():
                    own[m, 0] = total

                @pl.when(jnp.logical_not(settled))
                def _():
                    leaving[0, m] = total.astype(BF16)
                    z_beside(m).start()

            else:
                leaving[1, m] = total.astype(BF16)

                @pl.when(settled)
                def _():
                    z_across(m).start()

                @pl.when(jnp.logical_not(settled))
                def _():
                    z_corner(m).start()

    for m in range(2):
        z_across(m).wait_recv()
        at = pl.ds(m * PART, PART)

        @pl.when(settled)
        def _():
            normal[at, :] = (own[m, 0] + landed[0, m].astype(F32)) * scale

        @pl.when(jnp.logical_not(settled))
        def _():
            z_corner(m).wait_recv()
            normal[at, :] = (landed[0, m].astype(F32) + landed[1, m].astype(F32)) * scale

    @pl.when(o < 15)
    def _():
        for copy in halo_copies():
            copy.wait_send()

    for m in range(2):
        rows_over(m).wait_send()
        cols_over(m).wait_send()
        cols_across(m).wait_send()
        cols_on(m).wait_send()
        z_across(m).wait_send()

        @pl.when(jnp.logical_not(settled))
        def _():
            z_beside(m).wait_send()

        for rel in range(2):
            rows_up(m, rel).wait_send()
            rows_down(m, rel).wait_send()
            rows_on(m, rel).wait_send()
        for d in range(2):
            x_far(d, m).wait_send()
            x_raw(d, m).wait_send()
            x_sum(d, m).wait_send()
    for step in range(1, 16):
        rhs_to(step).wait_send()


def per_device(design, observed, row_weight, taps):
    total_rows = ROWS * lax.axis_size("obs")
    dma = pltpu.SemaphoreType.DMA
    vmem = pl.BlockSpec(memory_space=pltpu.VMEM)
    normal, rhs, filtered_obs = pl.pallas_call(
        functools.partial(kernel, 1.0 / total_rows, 1.0 / math.sqrt(total_rows)),
        out_shape=(
            jax.ShapeDtypeStruct((512, COLS), F32),
            jax.ShapeDtypeStruct((8, 128), F32),
            jax.ShapeDtypeStruct((1, ROWS), F32),
        ),
        in_specs=[vmem, vmem, vmem, pl.BlockSpec(memory_space=pltpu.SMEM)],
        out_specs=(vmem, vmem, vmem),
        scratch_shapes=[
            pltpu.VMEM((ROWS + 8, COLS), F32),
            pltpu.VMEM((16, COLS), BF16),
            pltpu.VMEM((8, 128), F32),
            pltpu.VMEM((8, 128), F32),
            pltpu.VMEM((ROWS, 128), F32),
            pltpu.VMEM((2, PART, ROWS), BF16),
            pltpu.VMEM((16, ROWS), BF16),
            pltpu.VMEM((4, 2, PART, DEPTH), BF16),
            pltpu.VMEM((2, 2, DEPTH, 512), BF16),
            pltpu.VMEM((3, 2, 2, PART, COLS), BF16),
            pltpu.VMEM((2, 2, PART, COLS), F32),
            pltpu.VMEM((2, 2, PART, COLS), BF16),
            pltpu.VMEM((2, 2, PART, COLS), BF16),
            pltpu.VMEM((2, PART, COLS), BF16),
            pltpu.VMEM((2, PART, COLS), BF16),
            pltpu.VMEM((2, 2, PART, COLS), BF16),
            pltpu.VMEM((2, 2, PART, COLS), BF16),
            pltpu.VMEM((16, 8, 128), F32),
            dma((2,)), dma((2,)),
            dma((2, 2, 2)), dma((2, 2)), dma((2,)), dma((4, 2, 2)),
            dma((2,)), dma((2,)), dma((2,)), dma((2, 2, 2)),
            dma((2, 3, 2)), dma((2, 3, 2)),
            dma((2, 2)), dma((2, 2)),
            dma((16,)), dma((16,)),
        ],
        compiler_params=pltpu.CompilerParams(collective_id=0, has_side_effects=True, vmem_limit_bytes=60 << 20),
        name="normal_equations",
    )(design, observed.reshape(1, ROWS), row_weight.reshape(1, ROWS), taps)
    return normal, rhs.reshape(COLS), filtered_obs.reshape(ROWS)


def solution(mesh):
    placed = (P("obs", "param"), P("obs"), P("obs"), P())
    return jax.shard_map(
        per_device,
        mesh=mesh,
        in_specs=placed,
        out_specs=(P("obs", "param"), P("param"), P("obs")),
        check_vma=False,
    )
```

```python
import functools
import math

import jax
import jax.numpy as jnp
from jax import lax
from jax.experimental import pallas as pl
from jax.experimental.pallas import tpu as pltpu
from jax.sharding import PartitionSpec as P

MESH = pl.DeviceIdType.MESH
BF16, F32 = jnp.bfloat16, jnp.float32
ROWS = 640
COLS = 1024
LAGS = 7
PART = 256
DEPTH = 2 * ROWS


def kernel(
    scale, rhs_scale,
    design, observed, weight, taps,
    normal, rhs, filtered_obs,
    ext, halo, obs_tail, obs_halo, wcol, mine, weighted, rows, cols, part, own, taken, far,
    leaving, landed, rhs_all,
    halo_s, halo_r, rows_s, rows_f, rows_sib, rows_r, cols_s, cols_sib, cols_f, cols_r, x_s, x_r, z_s, z_r, rhs_s, rhs_r,
):
    p, o = lax.axis_index("param"), lax.axis_index("obs")
    y, h = p // 2, p % 2
    x, l, k = o // 4, (o // 2) % 2, o % 2
    near = (y - x + 4) % 4
    settled = l == h

    def param_of(y_, h_):
        return ((y_ + 4) % 4) * 2 + h_

    def obs_of(x_, l_, k_):
        return ((x_ + 4) % 4) * 4 + l_ * 2 + k_

    sibling = (p, obs_of(x, l, 1 - k))
    across = (param_of(y, 1 - h), o)
    beside = (p, obs_of(x, 1 - l, k))
    corner = (param_of(y, 1 - h), obs_of(x, 1 - l, k))
    following = (p, (o + 1) % 16)

    def remote(src, dst, send, recv, device):
        return pltpu.make_async_remote_copy(
            src_ref=src, dst_ref=dst, send_sem=send, recv_sem=recv, device_id=device, device_id_type=MESH
        )

    def halo_copies():
        return (
            remote(design.at[pl.ds(ROWS - 16, 16), :], halo, halo_s.at[0], halo_r.at[0], following),
            remote(obs_tail, obs_halo, halo_s.at[1], halo_r.at[1], following),
        )

    def lanes(rel):
        return pl.ds(ROWS * rel, ROWS)

    def span(e):
        return pl.ds(0, PART) if e is None else pl.ds(pl.multiple_of(e * 128, 128), 128)

    def wide(c):
        return pl.ds(c * 512, 512)

    def rows_out(m, rel, e, up):
        target = (param_of(y + 2 * up - 1, h), obs_of(x, l, (k + rel) % 2))
        dy = 1 + 2 * up
        return remote(
            mine.at[rel, m, span(e)], rows.at[dy, m, span(e), lanes(rel)],
            rows_s.at[up, m, rel, e], rows_r.at[dy, m, rel, e], target,
        )

    def rows_on(m, rel, e):
        target = (param_of(y + 1 - 2 * m, h), o)
        return remote(
            rows.at[3 - 2 * m, m, span(e), lanes(rel)], rows.at[2, m, span(e), lanes(rel)],
            rows_f.at[m, rel, e], rows_r.at[2, m, rel, e], target,
        )

    def rows_at(dy, m, rel, e):
        piece = rows.at[dy, m, span(e), lanes(rel)]
        return remote(piece, piece, rows_f.at[0, 0, 0], rows_r.at[dy, m, rel, e], following)

    def rows_over(m, e):
        return remote(mine.at[1, m, span(e)], rows.at[0, m, span(e), lanes(1)], rows_sib.at[m, e], rows_r.at[0, m, 1, e], sibling)

    def cols_over(n):
        half = pl.ds(0, ROWS)
        return remote(cols.at[0, n, half, :], cols.at[0, n, pl.ds(ROWS, ROWS), :], cols_sib.at[n], cols_r.at[0, n, 1], sibling)

    def cols_across(n):
        half = pl.ds(0, ROWS)
        return remote(cols.at[0, n, half, :], cols.at[1, n, half, :], cols_s.at[n], cols_r.at[1, n, 0], across)

    def cols_on(n):
        half = pl.ds(0, ROWS)
        return remote(cols.at[1, n, half, :], cols.at[1, n, pl.ds(ROWS, ROWS), :], cols_f.at[n], cols_r.at[1, n, 1], sibling)

    def beyond(d):
        return (p, obs_of(x + 1 - 2 * d, l, k))

    def x_far(d, q, e=None):
        return remote(part.at[1, d, q, span(e)], far.at[d, q, span(e)], x_s.at[d, 0, q], x_r.at[d, 0, q], beyond(d))

    def x_raw(d, q, e=None):
        dst = taken.at[d, 1 - d, q, span(e)]
        return remote(part.at[2 * d, 1 - d, q, span(e)], dst, x_s.at[d, 1, q], x_r.at[d, 1, q], beyond(d))

    def x_sum(d, q):
        return remote(part.at[2 * d, d, q], taken.at[d, d, q], x_s.at[d, 2, q], x_r.at[d, 2, q], beyond(d))

    def z_home(m, c):
        return remote(leaving.at[0, m, c], landed.at[0, m, c], z_s.at[0, m, c], z_r.at[0, m, c], beside)

    def z_add(m, c):
        return remote(leaving.at[1, m, c], landed.at[1, m, c], z_s.at[1, m, c], z_r.at[1, m, c], beside)

    def z_on(m, c):
        return remote(leaving.at[1, m, c], landed.at[0, m, c], z_s.at[1, m, c], z_r.at[0, m, c], corner)

    def rhs_to(step):
        peer = (p, (o + step) % 16)
        return remote(rhs_all.at[o], rhs_all.at[o], rhs_s.at[step], rhs_r.at[step], peer)

    barrier = pltpu.get_barrier_semaphore()
    greeted = [(param_of(y + step, h), obs_of(x, l, core)) for step in (1, -1) for core in (k, 1 - k)] + [across, corner]
    greeted += [(p, (o + step) % 16) for step in range(1, 16)]
    for device in greeted:
        pl.semaphore_signal(barrier, inc=1, device_id=device, device_id_type=MESH)

    signal_row = jnp.broadcast_to(observed[...].astype(F32), (8, ROWS))
    weight_row = jnp.broadcast_to(weight[...], (8, ROWS))
    obs_tail[...] = signal_row[:, ROWS - 128 :]
    for r in range(ROWS // 128):
        block = jnp.broadcast_to(weight[:, r * 128 : (r + 1) * 128], (128, 128))
        wcol[pl.ds(r * 128, 128), :] = block.T

    def widen(i, _):
        at = pl.multiple_of(i * 128, 128)
        ext[pl.ds(8, ROWS), pl.ds(at, 128)] = design[:, pl.ds(at, 128)].astype(F32)
        return 0

    lax.fori_loop(0, COLS // 128, widen, 0)
    pl.semaphore_wait(barrier, len(greeted))

    @pl.when(o < 15)
    def _():
        for copy in halo_copies():
            copy.start()

    @pl.when(o > 0)
    def _():
        for copy in halo_copies():
            copy.wait_recv()
        ext[pl.ds(0, 8), :] = halo[...].astype(F32)[8:]

    @pl.when(o == 0)
    def _():
        ext[pl.ds(0, 8), :] = jnp.zeros((8, COLS), F32)
        obs_halo[...] = jnp.zeros((8, 128), F32)

    def first_pieces():
        return [rows_out(m, rel, e, 1 - m) for e in range(2) for m in range(2) for rel in (1, 0)]

    def second_pieces():
        return [rows_out(m, rel, e, m) for e in range(2) for m in range(2) for rel in (1, 0)]

    def passed_on(halves=(0, 1)):
        return [rows_on(m, rel, e) for e in halves for m in range(2) for rel in (1, 0)]

    def arrived(dy, m):
        for rel in (1, 0):
            for e in range(2):
                rows_at(dy, m, rel, e).wait_recv()

    def filter_block(i, _):
        e, m, rel = i // 4, (i // 2) % 2, 1 - i % 2
        core = (k + rel) % 2
        within = pl.multiple_of(m * PART + e * 128, 128)
        at = pl.ds(pl.multiple_of(core * 512 + within, 128), 128)
        for r in range(ROWS // 128):
            first = r * 128
            total = ext[pl.ds(8 + first, 128), at]
            for lag in range(1, LAGS + 1):
                total = total + taps[lag - 1] * ext[pl.ds(8 + first - lag, 128), at]
            rounded = total.astype(BF16).astype(F32)
            cols[0, core, pl.ds(first, 128), pl.ds(within, 128)] = (wcol[pl.ds(first, 128), :] * rounded).astype(BF16)
            turned = rounded.T.astype(BF16)
            mine[rel, m, span(e), pl.ds(first, 128)] = turned

            @pl.when(rel == 0)
            def _():
                rows[0, m, span(e), pl.ds(first, 128)] = turned

        rows_out(m, rel, e, 1 - m).start()

        @pl.when(rel == 1)
        def _():
            rows_over(m, e).start()

        return 0

    lax.fori_loop(0, 8, filter_block, 0)
    for n in range(2):
        cols_over(n).start()
        cols_across(n).start()
    first_far = near == 2

    @pl.when(first_far)
    def _():
        for copy in second_pieces():
            copy.start()

    extended = jnp.concatenate([obs_halo[...], signal_row], axis=1)
    total = signal_row
    for lag in range(1, LAGS + 1):
        total = total + taps[lag - 1] * pltpu.roll(extended, lag, 1)[:, 128:]
    filtered_obs[...] = total[0:1, :]
    weighted[...] = jnp.concatenate([weight_row * total, weight_row * total], axis=0).astype(BF16)
    line = lax.broadcasted_iota(jnp.int32, (8, 128), 0)
    sums = jnp.zeros((8, 128), F32)
    for m in range(2):
        for rel in range(2):
            core = (k + rel) % 2
            dots = lax.dot_general(weighted[...], mine[rel, m], (((1,), (1,)), ((), ())), preferred_element_type=F32)
            for c in range(2):
                sums = jnp.where(line == core * 4 + m * 2 + c, dots[0:8, c * 128 : (c + 1) * 128], sums)
    rhs_all[o] = sums
    for step in range(1, 16):
        rhs_to(step).start()

    def multiply(dy, m, q, e=None):
        role = (near + dy) % 4

        def chunk(c, _):
            at = pl.ds(pl.multiple_of(c * 256, 256), 256)
            value = jnp.dot(rows[dy, m, span(e)], cols[q // 2, q % 2, :, at], preferred_element_type=F32)

            @pl.when(role == 0)
            def _():
                own[m, q, span(e), at] = value

            @pl.when(role != 0)
            def _():
                part[role - 1, m, q, span(e), at] = value.astype(BF16)

            return 0

        lax.fori_loop(0, 2, chunk, 0)

        @pl.when(role == 2)
        def _():
            x_far(m, q, e).start()

        @pl.when(jnp.logical_or(jnp.logical_and(role == 1, m == 1), jnp.logical_and(role == 3, m == 0)))
        def _():
            x_raw(role // 2, q, e).start()

    def add_far(d, q, valid=True):
        @pl.when(valid)
        def _():
            x_far(d, q).wait_recv()
            part[2 * d, d, q] = (part[2 * d, d, q].astype(F32) + far[d, q].astype(F32)).astype(BF16)
            x_sum(d, q).start()

    def by_near(*values):
        chosen = values[3]
        for place in (2, 1, 0):
            chosen = jnp.where(near == place, values[place], chosen)
        return chosen

    for m in range(2):
        for e in range(2):
            rows_over(m, e).wait_recv()
        cols_over(m).wait_recv()
    for q in range(2):
        for m in (1, 0):
            multiply(0, m, q)

    for e in range(2):
        for m in range(2):
            for rel in (1, 0):
                rows_at(3 - 2 * m, m, rel, e).wait_recv()
        for copy in passed_on((e,)):
            copy.start()
        if e == 1:

            @pl.when(jnp.logical_not(first_far))
            def _():
                for copy in second_pieces():
                    copy.start()

        for q in range(2):
            multiply(3, 0, q, e)
            multiply(1, 1, q, e)
        add_far(by_near(0, 0, 0, 1), e, (near % 2) == 1)
    cols_across(0).wait_recv()
    cols_on(0).start()
    cols_on(0).wait_recv()
    for m in (1, 0):
        multiply(0, m, 2)
    multiply(3, 0, 2)
    multiply(1, 1, 2)
    for q in range(2):
        for d in range(2):
            add_far(d, q, near == 2)
    add_far(by_near(0, 0, 0, 1), 2, (near % 2) == 1)

    third = (by_near(2, 1, 2, 3), by_near(0, 0, 0, 1))
    fourth = (2, by_near(1, 0, 1, 1))
    fifth = (by_near(1, 2, 1, 2), by_near(0, 1, 0, 0))
    sixth = (by_near(3, 3, 3, 1), by_near(1, 1, 1, 0))
    arrived(*third)
    multiply(*third, 0)
    arrived(*fourth)
    multiply(*fourth, 0)
    for q in (1, 2):
        multiply(*third, q)
        multiply(*fourth, q)
    cols_across(1).wait_recv()
    cols_on(1).start()
    cols_on(1).wait_recv()
    multiply(*third, 3)
    multiply(*fourth, 3)
    for m in (1, 0):
        multiply(0, m, 3)
    multiply(3, 0, 3)
    multiply(1, 1, 3)

    add_far(by_near(0, 0, 0, 1), by_near(0, 3, 2, 3), near != 0)
    add_far(1, 2, near == 2)

    for piece in (fifth, sixth):
        arrived(*piece)
    for q in (0, 2, 3, 1):
        for piece in (fifth, sixth):
            multiply(*piece, q)
    for q in (0, 2, 3, 1):
        add_far(by_near(0, 1, 0, 0), q, jnp.logical_or(near != 2, q == 3))
        add_far(1, q, jnp.logical_or(near == 0, jnp.logical_and(near == 2, q == 3)))

    for step in range(1, 16):
        rhs_to(step).wait_recv()
    total = rhs_all[0]
    for step in range(1, 16):
        total = total + rhs_all[step]
    rhs[...] = total * rhs_scale

    def summed(m, q):
        x_sum(m, q).wait_recv()
        x_raw(1 - m, q).wait_recv()
        return own[m, q] + taken[0, m, q].astype(F32) + taken[1, m, q].astype(F32)

    def keep_near(c):
        for m in range(2):
            total = summed(m, c)

            @pl.when(settled)
            def _():
                own[m, c] = total

            @pl.when(jnp.logical_not(settled))
            def _():
                leaving[0, m, c] = total.astype(BF16)
                z_home(m, c).start()

    def pass_over(c):
        for m in range(2):
            total = summed(m, 2 + c)

            @pl.when(settled)
            def _():
                leaving[1, m, c] = total.astype(BF16)
                z_add(m, c).start()

            @pl.when(jnp.logical_not(settled))
            def _():
                own[m, 2 + c] = total

    def pass_on(c):
        @pl.when(jnp.logical_not(settled))
        def _():
            for m in range(2):
                z_add(m, c).wait_recv()
                leaving[1, m, c] = (own[m, 2 + c] + landed[1, m, c].astype(F32)).astype(BF16)
                z_on(m, c).start()

    keep_near(0)
    pass_over(0)
    pass_over(1)
    pass_on(0)
    keep_near(1)
    pass_on(1)

    for c in range(2):
        for m in range(2):
            z_home(m, c).wait_recv()
            at = pl.ds(m * PART, PART)

            @pl.when(settled)
            def _():
                normal[at, wide(c)] = (own[m, c] + landed[0, m, c].astype(F32)) * scale

            @pl.when(jnp.logical_not(settled))
            def _():
                normal[at, wide(c)] = landed[0, m, c].astype(F32) * scale

    @pl.when(o < 15)
    def _():
        for copy in halo_copies():
            copy.wait_send()

    for m in range(2):
        for e in range(2):
            rows_over(m, e).wait_send()
        cols_over(m).wait_send()
        cols_across(m).wait_send()
        cols_on(m).wait_send()
        for c in range(2):
            z_add(m, c).wait_send()

        @pl.when(jnp.logical_not(settled))
        def _():
            for c in range(2):
                z_home(m, c).wait_send()

        for q in range(4):
            x_far(m, q).wait_send()
            x_raw(m, q).wait_send()
            x_sum(m, q).wait_send()
    for copy in first_pieces() + passed_on() + second_pieces():
        copy.wait_send()
    for step in range(1, 16):
        rhs_to(step).wait_send()


def per_device(design, observed, row_weight, taps):
    total_rows = ROWS * lax.axis_size("obs")
    dma = pltpu.SemaphoreType.DMA
    vmem = pl.BlockSpec(memory_space=pltpu.VMEM)
    normal, rhs, filtered_obs = pl.pallas_call(
        functools.partial(kernel, 1.0 / total_rows, 1.0 / math.sqrt(total_rows)),
        out_shape=(
            jax.ShapeDtypeStruct((512, COLS), F32),
            jax.ShapeDtypeStruct((8, 128), F32),
            jax.ShapeDtypeStruct((1, ROWS), F32),
        ),
        in_specs=[vmem, vmem, vmem, pl.BlockSpec(memory_space=pltpu.SMEM)],
        out_specs=(vmem, vmem, vmem),
        scratch_shapes=[
            pltpu.VMEM((ROWS + 8, COLS), F32),
            pltpu.VMEM((16, COLS), BF16),
            pltpu.VMEM((8, 128), F32),
            pltpu.VMEM((8, 128), F32),
            pltpu.VMEM((ROWS, 128), F32),
            pltpu.VMEM((2, 2, PART, ROWS), BF16),
            pltpu.VMEM((16, ROWS), BF16),
            pltpu.VMEM((4, 2, PART, DEPTH), BF16),
            pltpu.VMEM((2, 2, DEPTH, 512), BF16),
            pltpu.VMEM((3, 2, 4, PART, 512), BF16),
            pltpu.VMEM((2, 4, PART, 512), F32),
            pltpu.VMEM((2, 2, 4, PART, 512), BF16),
            pltpu.VMEM((2, 4, PART, 512), BF16),
            pltpu.VMEM((2, 2, 2, PART, 512), BF16),
            pltpu.VMEM((2, 2, 2, PART, 512), BF16),
            pltpu.VMEM((16, 8, 128), F32),
            dma((2,)), dma((2,)),
            dma((2, 2, 2, 2)), dma((2, 2, 2)), dma((2, 2)), dma((4, 2, 2, 2)),
            dma((2,)), dma((2,)), dma((2,)), dma((2, 2, 2)),
            dma((2, 3, 4)), dma((2, 3, 4)),
            dma((2, 2, 2)), dma((2, 2, 2)),
            dma((16,)), dma((16,)),
        ],
        compiler_params=pltpu.CompilerParams(collective_id=0, has_side_effects=True, vmem_limit_bytes=60 << 20),
        name="normal_equations",
    )(design, observed.reshape(1, ROWS), row_weight.reshape(1, ROWS), taps)
    return normal, rhs.reshape(COLS), filtered_obs.reshape(ROWS)


def solution(mesh):
    placed = (P("obs", "param"), P("obs"), P("obs"), P())
    return jax.shard_map(
        per_device,
        mesh=mesh,
        in_specs=placed,
        out_specs=(P("obs", "param"), P("param"), P("obs")),
        check_vma=False,
    )
```

```python
import functools
import math

import jax
import jax.numpy as jnp
from jax import lax
from jax.experimental import pallas as pl
from jax.experimental.pallas import tpu as pltpu
from jax.sharding import PartitionSpec as P

MESH = pl.DeviceIdType.MESH
BF16, F32 = jnp.bfloat16, jnp.float32
ROWS = 640
COLS = 1024
LAGS = 7
PART = 256
DEPTH = 2 * ROWS


def kernel(
    scale, rhs_scale,
    design_hbm, observed, weight, taps,
    normal, rhs, filtered_obs,
    design, ext, halo, obs_tail, obs_halo, wcol, mine, weighted, rows, cols, part, own, taken, far,
    leaving, landed, passing, rhs_all,
    design_s, halo_s, halo_r, rows_s, rows_f, rows_sib, rows_r, cols_s, cols_sib, cols_f, cols_r, x_s, x_r, z_s, z_r, z_fs, z_fr, rhs_s, rhs_r,
):
    p, o = lax.axis_index("param"), lax.axis_index("obs")
    y, h = p // 2, p % 2
    x, l, k = o // 4, (o // 2) % 2, o % 2
    near = (y - x + 4) % 4
    settled = l == h

    def param_of(y_, h_):
        return ((y_ + 4) % 4) * 2 + h_

    def obs_of(x_, l_, k_):
        return ((x_ + 4) % 4) * 4 + l_ * 2 + k_

    sibling = (p, obs_of(x, l, 1 - k))
    across = (param_of(y, 1 - h), o)
    beside = (p, obs_of(x, 1 - l, k))
    corner = (param_of(y, 1 - h), obs_of(x, 1 - l, k))
    following = (p, (o + 1) % 16)

    def remote(src, dst, send, recv, device):
        return pltpu.make_async_remote_copy(
            src_ref=src, dst_ref=dst, send_sem=send, recv_sem=recv, device_id=device, device_id_type=MESH
        )

    def halo_copies():
        return (
            remote(design.at[pl.ds(ROWS - 16, 16), :], halo, halo_s.at[0], halo_r.at[0], following),
            remote(obs_tail, obs_halo, halo_s.at[1], halo_r.at[1], following),
        )

    def lanes(rel):
        return pl.ds(ROWS * rel, ROWS)

    def span(e):
        return pl.ds(0, PART) if e is None else pl.ds(pl.multiple_of(e * 128, 128), 128)

    def wide(c):
        return pl.ds(c * 512, 512)

    def rows_out(m, rel, e, up):
        target = (param_of(y + 2 * up - 1, h), obs_of(x, l, (k + rel) % 2))
        dy = 1 + 2 * up
        return remote(
            mine.at[rel, m, span(e)], rows.at[dy, m, span(e), lanes(rel)],
            rows_s.at[up, m, rel, e], rows_r.at[dy, m, rel, e], target,
        )

    def rows_on(m, rel, e):
        target = (param_of(y + 1 - 2 * m, h), o)
        return remote(
            rows.at[3 - 2 * m, m, span(e), lanes(rel)], rows.at[2, m, span(e), lanes(rel)],
            rows_f.at[m, rel, e], rows_r.at[2, m, rel, e], target,
        )

    def rows_at(dy, m, rel, e):
        piece = rows.at[dy, m, span(e), lanes(rel)]
        return remote(piece, piece, rows_f.at[0, 0, 0], rows_r.at[dy, m, rel, e], following)

    def rows_over(m, e):
        return remote(mine.at[1, m, span(e)], rows.at[0, m, span(e), lanes(1)], rows_sib.at[m, e], rows_r.at[0, m, 1, e], sibling)

    def cols_over(n):
        half = pl.ds(0, ROWS)
        return remote(cols.at[0, n, half, :], cols.at[0, n, pl.ds(ROWS, ROWS), :], cols_sib.at[n], cols_r.at[0, n, 1], sibling)

    def cols_across(n):
        half = pl.ds(0, ROWS)
        return remote(cols.at[0, n, half, :], cols.at[1, n, half, :], cols_s.at[n], cols_r.at[1, n, 0], across)

    def cols_on(n):
        half = pl.ds(0, ROWS)
        return remote(cols.at[1, n, half, :], cols.at[1, n, pl.ds(ROWS, ROWS), :], cols_f.at[n], cols_r.at[1, n, 1], sibling)

    def beyond(d):
        return (p, obs_of(x + 1 - 2 * d, l, k))

    def x_far(d, q, e=None):
        return remote(part.at[1, d, q, span(e)], far.at[d, q, span(e)], x_s.at[d, 0, q], x_r.at[d, 0, q], beyond(d))

    def x_raw(d, q, e=None):
        dst = taken.at[d, 1 - d, q, span(e)]
        return remote(part.at[2 * d, 1 - d, q, span(e)], dst, x_s.at[d, 1, q], x_r.at[d, 1, q], beyond(d))

    def x_sum(d, q, e=None):
        kind = 2 if e is None else 2 + e
        return remote(
            part.at[2 * d, d, q, span(e)], taken.at[d, d, q, span(e)], x_s.at[d, kind, q], x_r.at[d, kind, q], beyond(d)
        )

    def z_home(m, c, e=None):
        sem = c if e is None else c + e
        return remote(leaving.at[0, m, c, span(e)], landed.at[0, m, c, span(e)], z_s.at[0, m, sem], z_r.at[0, m, sem], beside)

    def z_add(c):
        return remote(leaving.at[1, 0, c], landed.at[1, 0, c], z_s.at[1, 0, c], z_r.at[1, 0, c], beside)

    def z_on(m, c):
        return remote(leaving.at[1, m, c], landed.at[0, m, c], z_s.at[1, m, c], z_r.at[0, m, c], corner)

    def z_via(c):
        return remote(leaving.at[1, 1, c], passing.at[c], z_s.at[1, 1, c], z_r.at[1, 1, c], corner)

    def z_fwd(c):
        return remote(passing.at[c], landed.at[1, 1, c], z_fs.at[c], z_fr.at[c], beside)

    def rhs_to(step):
        peer = (p, (o + step) % 16)
        return remote(rhs_all.at[o], rhs_all.at[o], rhs_s.at[step], rhs_r.at[step], peer)

    incoming = pltpu.make_async_copy(design_hbm, design, design_s)
    incoming.start()

    barrier = pltpu.get_barrier_semaphore()
    greeted = [(param_of(y + step, h), obs_of(x, l, core)) for step in (1, -1) for core in (k, 1 - k)] + [across, corner]
    greeted += [(p, (o + step) % 16) for step in range(1, 16)]
    for device in greeted:
        pl.semaphore_signal(barrier, inc=1, device_id=device, device_id_type=MESH)

    signal_row = jnp.broadcast_to(observed[...].astype(F32).reshape(1, ROWS), (8, ROWS))
    weight_row = jnp.broadcast_to(weight[...].reshape(1, ROWS), (8, ROWS))
    obs_tail[...] = signal_row[:, ROWS - 128 :]
    for r in range(ROWS // 128):
        block = jnp.broadcast_to(weight_row[0:1, r * 128 : (r + 1) * 128], (128, 128))
        wcol[pl.ds(r * 128, 128), :] = block.T

    def widen(i, _):
        at = pl.multiple_of(i * 128, 128)
        ext[pl.ds(8, ROWS), pl.ds(at, 128)] = design[:, pl.ds(at, 128)].astype(F32)
        return 0

    incoming.wait()
    lax.fori_loop(0, COLS // 128, widen, 0)

    def filter_rows(i, r):
        e, m, rel = i // 4, (i // 2) % 2, 1 - i % 2
        core = (k + rel) % 2
        at = pl.ds(pl.multiple_of(core * 512 + m * PART + e * 128, 128), 128)
        quarter = pl.ds(pl.multiple_of((core * 2 + m) * 128, 128), 128)
        first = r * 128
        total = ext[pl.ds(8 + first, 128), at]
        for lag in range(1, LAGS + 1):
            total = total + taps[lag - 1] * ext[pl.ds(8 + first - lag, 128), at]
        rounded = total.astype(BF16).astype(F32)
        cols[0, e, pl.ds(first, 128), quarter] = (wcol[pl.ds(first, 128), :] * rounded).astype(BF16)
        turned = rounded.T.astype(BF16)
        mine[rel, m, span(e), pl.ds(first, 128)] = turned

        @pl.when(rel == 0)
        def _():
            rows[0, m, span(e), pl.ds(first, 128)] = turned

    def filter_later_rows(i, _):
        for r in range(1, ROWS // 128):
            filter_rows(i, r)
        return 0

    lax.fori_loop(0, 4, filter_later_rows, 0)
    pl.semaphore_wait(barrier, len(greeted))

    @pl.when(o < 15)
    def _():
        for copy in halo_copies():
            copy.start()

    lax.fori_loop(4, 8, filter_later_rows, 0)

    @pl.when(o > 0)
    def _():
        for copy in halo_copies():
            copy.wait_recv()
        ext[pl.ds(0, 8), :] = halo[...].astype(F32)[8:]

    @pl.when(o == 0)
    def _():
        ext[pl.ds(0, 8), :] = jnp.zeros((8, COLS), F32)
        obs_halo[...] = jnp.zeros((8, 128), F32)

    def first_pieces():
        return [rows_out(m, rel, e, 1 - m) for e in range(2) for m in range(2) for rel in (1, 0)]

    def second_pieces():
        return [rows_out(m, rel, e, m) for e in range(2) for m in range(2) for rel in (1, 0)]

    def passed_on(halves=(0, 1)):
        return [rows_on(m, rel, e) for e in halves for m in range(2) for rel in (1, 0)]

    def arrived(dy, m):
        for rel in (1, 0):
            for e in range(2):
                rows_at(dy, m, rel, e).wait_recv()

    def filter_block(i, _):
        e, m, rel = i // 4, (i // 2) % 2, 1 - i % 2
        filter_rows(i, 0)
        rows_out(m, rel, e, 1 - m).start()

        @pl.when(rel == 1)
        def _():
            rows_over(m, e).start()

        @pl.when(i == 3)
        def _():
            cols_over(0).start()
            cols_across(0).start()

        return 0

    lax.fori_loop(0, 8, filter_block, 0)
    cols_over(1).start()
    cols_across(1).start()
    first_far = near == 2

    @pl.when(first_far)
    def _():
        for copy in second_pieces():
            copy.start()

    def multiply(dy, m, q, e=None):
        role = (near + dy) % 4

        def chunk(c, _):
            at = pl.ds(pl.multiple_of(c * 256, 256), 256)
            value = jnp.dot(rows[dy, m, span(e)], cols[q // 2, q % 2, :, at], preferred_element_type=F32)

            @pl.when(role == 0)
            def _():
                own[m, q, span(e), at] = value

            @pl.when(role != 0)
            def _():
                part[role - 1, m, q, span(e), at] = value.astype(BF16)

            return 0

        lax.fori_loop(0, 2, chunk, 0)

        @pl.when(role == 2)
        def _():
            x_far(m, q, e).start()

        @pl.when(jnp.logical_or(jnp.logical_and(role == 1, m == 1), jnp.logical_and(role == 3, m == 0)))
        def _():
            x_raw(role // 2, q, e).start()

    def add_far(d, q, valid=True):
        @pl.when(valid)
        def _():
            x_far(d, q).wait_recv()
            for e in halves_of(q):
                both = part[2 * d, d, q, span(e)].astype(F32) + far[d, q, span(e)].astype(F32)
                part[2 * d, d, q, span(e)] = both.astype(BF16)
                x_sum(d, q, e).start()

    def halves_of(q):
        return (0, 1) if isinstance(q, int) and q == 1 else (None,)

    def by_near(*values):
        chosen = values[3]
        for place in (2, 1, 0):
            chosen = jnp.where(near == place, values[place], chosen)
        return chosen

    for m in range(2):
        for e in range(2):
            rows_over(m, e).wait_recv()
        cols_over(m).wait_recv()
    for q in range(2):
        for m in (1, 0):
            multiply(0, m, q)

    for e in range(2):
        for m in range(2):
            for rel in (1, 0):
                rows_at(3 - 2 * m, m, rel, e).wait_recv()
        for copy in passed_on((e,)):
            copy.start()
        if e == 1:

            @pl.when(jnp.logical_not(first_far))
            def _():
                for copy in second_pieces():
                    copy.start()

        for q in range(2):
            multiply(3, 0, q, e)
            multiply(1, 1, q, e)
        add_far(by_near(0, 0, 0, 1), e, (near % 2) == 1)
    cols_across(0).wait_recv()
    cols_on(0).start()
    cols_on(0).wait_recv()
    multiply(by_near(3, 0, 0, 0), by_near(0, 1, 1, 1), 2)
    multiply(by_near(1, 0, 0, 0), by_near(1, 0, 0, 0), 2)
    multiply(by_near(0, 3, 3, 3), by_near(1, 0, 0, 0), 2)
    multiply(by_near(0, 1, 1, 1), by_near(0, 1, 1, 1), 2)
    for q in range(2):
        for d in range(2):
            add_far(d, q, near == 2)

    extended = jnp.concatenate([obs_halo[...], signal_row], axis=1)
    total = signal_row
    for lag in range(1, LAGS + 1):
        total = total + taps[lag - 1] * pltpu.roll(extended, lag, 1)[:, 128:]
    filtered_obs[...] = total[0:1, :].reshape(ROWS)
    weighted[...] = jnp.concatenate([weight_row * total, weight_row * total], axis=0).astype(BF16)
    line = lax.broadcasted_iota(jnp.int32, (8, 128), 0)
    sums = jnp.zeros((8, 128), F32)
    for m in range(2):
        for rel in range(2):
            core = (k + rel) % 2
            dots = lax.dot_general(weighted[...], mine[rel, m], (((1,), (1,)), ((), ())), preferred_element_type=F32)
            for c in range(2):
                sums = jnp.where(line == core * 4 + m * 2 + c, dots[0:8, c * 128 : (c + 1) * 128], sums)
    rhs_all[o] = sums
    for step in range(1, 16):
        rhs_to(step).start()

    third = (by_near(2, 1, 2, 3), by_near(0, 0, 0, 1))
    fourth = (2, by_near(1, 0, 1, 1))
    fifth = (by_near(1, 2, 1, 2), by_near(0, 1, 0, 0))
    sixth = (by_near(3, 3, 3, 1), by_near(1, 1, 1, 0))
    arrived(*third)
    multiply(*third, 0)
    arrived(*fourth)
    multiply(*fourth, 0)
    multiply(*third, 2)
    multiply(*fourth, 2)
    cols_across(1).wait_recv()
    cols_on(1).start()
    cols_on(1).wait_recv()

    def last_sums(q, valid=True):
        add_far(by_near(0, 1, 0, 0), q, valid)
        add_far(1, q, jnp.logical_and(valid, (near % 2) == 0))

    multiply(by_near(2, 1, 0, 3), by_near(0, 0, 1, 1), 3)
    multiply(by_near(2, 1, 0, 3), by_near(1, 1, 0, 0), 3)
    add_far(by_near(0, 0, 0, 1), 2, near != 0)
    add_far(1, 2, near == 2)
    multiply(by_near(3, 0, 3, 0), by_near(0, 0, 0, 1), 3)
    multiply(by_near(1, 0, 1, 0), by_near(1, 1, 1, 0), 3)

    @pl.when(near != 0)
    def _():
        multiply(*third, 1)
        multiply(*fourth, 1)

    multiply(by_near(0, 2, 2, 2), by_near(0, 0, 0, 1), 3)
    multiply(by_near(0, 3, 2, 1), by_near(1, 0, 1, 1), 3)
    for piece in (fifth, sixth):
        arrived(*piece)
    for q in (0, 2):
        for piece in (fifth, sixth):
            multiply(*piece, q)
        last_sums(q, near != 2)
    add_far(by_near(0, 0, 0, 1), 3, (near % 2) == 1)
    for piece in (fifth, sixth):
        multiply(*piece, 3)

    @pl.when(near == 0)
    def _():
        multiply(*third, 1)
        multiply(*fourth, 1)

    last_sums(3)
    for piece in (fifth, sixth):
        multiply(*piece, 1)
    last_sums(1, near == 0)

    for step in range(1, 16):
        rhs_to(step).wait_recv()
    total = rhs_all[0]
    for step in range(1, 16):
        total = total + rhs_all[step]
    rhs[...] = (total * rhs_scale).reshape(COLS)

    def summed(m, q, e=None):
        x_sum(m, q, e).wait_recv()
        if not e:
            x_raw(1 - m, q).wait_recv()
        return own[m, q, span(e)] + taken[0, m, q, span(e)].astype(F32) + taken[1, m, q, span(e)].astype(F32)

    def keep_near(c):
        for e in halves_of(c):
            for m in range(2):
                total = summed(m, c, e)

                @pl.when(settled)
                def _():
                    own[m, c, span(e)] = total

                @pl.when(jnp.logical_not(settled))
                def _():
                    leaving[0, m, c, span(e)] = total.astype(BF16)
                    z_home(m, c, e).start()

    def pass_over(c):
        for m in (1, 0):
            total = summed(m, 2 + c)

            @pl.when(settled)
            def _():
                leaving[1, m, c] = total.astype(BF16)
                (z_add(c) if m == 0 else z_via(c)).start()

            @pl.when(jnp.logical_not(settled))
            def _():
                if m == 0:
                    own[m, 2 + c] = total
                else:
                    leaving[1, m, c] = total.astype(BF16)
                    z_on(m, c).start()

    def pass_on(c):
        @pl.when(settled)
        def _():
            z_via(c).wait_recv()
            z_fwd(c).start()

        @pl.when(jnp.logical_not(settled))
        def _():
            z_add(c).wait_recv()
            leaving[1, 0, c] = (own[0, 2 + c] + landed[1, 0, c].astype(F32)).astype(BF16)
            z_on(0, c).start()

    keep_near(0)
    pass_over(0)
    last_sums(1, (near % 2) == 1)
    pass_over(1)
    pass_on(0)
    keep_near(1)
    pass_on(1)

    def place(m, c, total):
        for b in range(4):
            to = pl.ds(b // 2 * 512 + b % 2 * 256 + c * 128, 128)
            normal[pl.ds(m * PART, PART), to] = total[:, b * 128 : b * 128 + 128] * scale

    for c in range(2):
        for m in range(2):

            @pl.when(settled)
            def _():
                for e in halves_of(c):
                    z_home(m, c, e).wait_recv()
                place(m, c, own[m, c] + landed[0, m, c].astype(F32))

            @pl.when(jnp.logical_not(settled))
            def _():
                z_on(m, c).wait_recv()
                total = landed[0, m, c].astype(F32)
                if m == 1:
                    z_fwd(c).wait_recv()
                    total = total + landed[1, 1, c].astype(F32)
                place(m, c, total)

    @pl.when(o < 15)
    def _():
        for copy in halo_copies():
            copy.wait_send()

    for m in range(2):
        for e in range(2):
            rows_over(m, e).wait_send()
        cols_over(m).wait_send()
        cols_across(m).wait_send()
        cols_on(m).wait_send()
        for c in range(2):
            z_on(m, c).wait_send()

            @pl.when(jnp.logical_not(settled))
            def _():
                for e in halves_of(c):
                    z_home(m, c, e).wait_send()

        @pl.when(settled)
        def _():
            z_fwd(m).wait_send()

        for q in range(4):
            x_far(m, q).wait_send()
            x_raw(m, q).wait_send()
            for e in halves_of(q):
                x_sum(m, q, e).wait_send()
    for copy in first_pieces() + passed_on() + second_pieces():
        copy.wait_send()
    for step in range(1, 16):
        rhs_to(step).wait_send()


def per_device(design, observed, row_weight, taps):
    total_rows = ROWS * lax.axis_size("obs")
    dma = pltpu.SemaphoreType.DMA
    vmem = pl.BlockSpec(memory_space=pltpu.VMEM)
    normal, rhs, filtered_obs = pl.pallas_call(
        functools.partial(kernel, 1.0 / total_rows, 1.0 / math.sqrt(total_rows)),
        out_shape=(
            jax.ShapeDtypeStruct((512, COLS), F32),
            jax.ShapeDtypeStruct((COLS,), F32),
            jax.ShapeDtypeStruct((ROWS,), F32),
        ),
        in_specs=[pl.BlockSpec(memory_space=pl.ANY), vmem, vmem, pl.BlockSpec(memory_space=pltpu.SMEM)],
        out_specs=(vmem, vmem, vmem),
        scratch_shapes=[
            pltpu.VMEM((ROWS, COLS), BF16),
            pltpu.VMEM((ROWS + 8, COLS), F32),
            pltpu.VMEM((16, COLS), BF16),
            pltpu.VMEM((8, 128), F32),
            pltpu.VMEM((8, 128), F32),
            pltpu.VMEM((ROWS, 128), F32),
            pltpu.VMEM((2, 2, PART, ROWS), BF16),
            pltpu.VMEM((16, ROWS), BF16),
            pltpu.VMEM((4, 2, PART, DEPTH), BF16),
            pltpu.VMEM((2, 2, DEPTH, 512), BF16),
            pltpu.VMEM((3, 2, 4, PART, 512), BF16),
            pltpu.VMEM((2, 4, PART, 512), F32),
            pltpu.VMEM((2, 2, 4, PART, 512), BF16),
            pltpu.VMEM((2, 4, PART, 512), BF16),
            pltpu.VMEM((2, 2, 2, PART, 512), BF16),
            pltpu.VMEM((2, 2, 2, PART, 512), BF16),
            pltpu.VMEM((2, PART, 512), BF16),
            pltpu.VMEM((16, 8, 128), F32),
            dma, dma((2,)), dma((2,)),
            dma((2, 2, 2, 2)), dma((2, 2, 2)), dma((2, 2)), dma((4, 2, 2, 2)),
            dma((2,)), dma((2,)), dma((2,)), dma((2, 2, 2)),
            dma((2, 4, 4)), dma((2, 4, 4)),
            dma((2, 2, 3)), dma((2, 2, 3)), dma((2,)), dma((2,)),
            dma((16,)), dma((16,)),
        ],
        compiler_params=pltpu.CompilerParams(collective_id=0, has_side_effects=True, vmem_limit_bytes=60 << 20),
        name="normal_equations",
    )(design, observed, row_weight, taps)
    return normal, rhs, filtered_obs


def solution(mesh):
    placed = (P("obs", "param"), P("obs"), P("obs"), P())
    return jax.shard_map(
        per_device,
        mesh=mesh,
        in_specs=placed,
        out_specs=(P("obs", "param"), P("param"), P("obs")),
        check_vma=False,
    )
```

```python
import functools
import math

import jax
import jax.numpy as jnp
from jax import lax
from jax.experimental import pallas as pl
from jax.experimental.pallas import tpu as pltpu
from jax.sharding import PartitionSpec as P

MESH = pl.DeviceIdType.MESH
BF16, F32 = jnp.bfloat16, jnp.float32
ROWS = 640
COLS = 1024
LAGS = 7
PART = 256
DEPTH = 2 * ROWS


def kernel(
    scale, rhs_scale,
    design_hbm, observed, weight, taps,
    normal, rhs, filtered_obs,
    design, ext, halo, obs_tail, obs_halo, wcol, mine, weighted, rows, cols, part, own, taken, far,
    leaving, landed, passing, rhs_all,
    design_s, halo_s, halo_r, rows_s, rows_f, rows_sib, rows_r, cols_s, cols_sib, cols_f, cols_r, x_s, x_r, z_s, z_r, z_fs, z_fr, rhs_s, rhs_r,
):
    p, o = lax.axis_index("param"), lax.axis_index("obs")
    y, h = p // 2, p % 2
    x, l, k = o // 4, (o // 2) % 2, o % 2
    near = (y - x + 4) % 4
    settled = l == h

    def param_of(y_, h_):
        return ((y_ + 4) % 4) * 2 + h_

    def obs_of(x_, l_, k_):
        return ((x_ + 4) % 4) * 4 + l_ * 2 + k_

    sibling = (p, obs_of(x, l, 1 - k))
    across = (param_of(y, 1 - h), o)
    beside = (p, obs_of(x, 1 - l, k))
    corner = (param_of(y, 1 - h), obs_of(x, 1 - l, k))
    following = (p, (o + 1) % 16)

    def remote(src, dst, send, recv, device):
        return pltpu.make_async_remote_copy(
            src_ref=src, dst_ref=dst, send_sem=send, recv_sem=recv, device_id=device, device_id_type=MESH
        )

    def halo_copies():
        return (
            remote(design.at[pl.ds(ROWS - 16, 16), :], halo, halo_s.at[0], halo_r.at[0], following),
            remote(obs_tail, obs_halo, halo_s.at[1], halo_r.at[1], following),
        )

    def lanes(rel):
        return pl.ds(ROWS * rel, ROWS)

    def span(e):
        return pl.ds(0, PART) if e is None else pl.ds(pl.multiple_of(e * 128, 128), 128)

    def wide(c):
        return pl.ds(c * 512, 512)

    def rows_out(m, rel, e, up, begin=0, end=ROWS):
        target = (param_of(y + 2 * up - 1, h), obs_of(x, l, (k + rel) % 2))
        dy = 1 + 2 * up
        to = pl.ds(pl.multiple_of(ROWS * rel + begin, 128), end - begin)
        return remote(
            mine.at[rel, m, span(e), pl.ds(begin, end - begin)], rows.at[dy, m, span(e), to],
            rows_s.at[up, m, rel, e], rows_r.at[dy, m, rel, e], target,
        )

    def rows_on(m, rel, e):
        target = (param_of(y + 1 - 2 * m, h), o)
        return remote(
            rows.at[3 - 2 * m, m, span(e), lanes(rel)], rows.at[2, m, span(e), lanes(rel)],
            rows_f.at[m, rel, e], rows_r.at[2, m, rel, e], target,
        )

    def rows_at(dy, m, rel, e):
        piece = rows.at[dy, m, span(e), lanes(rel)]
        return remote(piece, piece, rows_f.at[0, 0, 0], rows_r.at[dy, m, rel, e], following)

    def rows_over(m, e):
        return remote(mine.at[1, m, span(e)], rows.at[0, m, span(e), lanes(1)], rows_sib.at[m, e], rows_r.at[0, m, 1, e], sibling)

    def cols_over(n, begin=0, end=ROWS):
        half, other = pl.ds(begin, end - begin), pl.ds(ROWS + begin, end - begin)
        return remote(cols.at[0, n, half, :], cols.at[0, n, other, :], cols_sib.at[n], cols_r.at[0, n, 1], sibling)

    def cols_across(n, begin=0, end=ROWS):
        half = pl.ds(begin, end - begin)
        return remote(cols.at[0, n, half, :], cols.at[1, n, half, :], cols_s.at[n], cols_r.at[1, n, 0], across)

    def cols_on(n):
        half = pl.ds(0, ROWS)
        return remote(cols.at[1, n, half, :], cols.at[1, n, pl.ds(ROWS, ROWS), :], cols_f.at[n], cols_r.at[1, n, 1], sibling)

    def beyond(d):
        return (p, obs_of(x + 1 - 2 * d, l, k))

    def x_far(d, q, e=None):
        return remote(part.at[1, d, q, span(e)], far.at[d, q, span(e)], x_s.at[d, 0, q], x_r.at[d, 0, q], beyond(d))

    def x_raw(d, q, e=None):
        dst = taken.at[d, 1 - d, q, span(e)]
        return remote(part.at[2 * d, 1 - d, q, span(e)], dst, x_s.at[d, 1, q], x_r.at[d, 1, q], beyond(d))

    def x_sum(d, q, e=None):
        kind = 2 if e is None else 2 + e
        return remote(
            part.at[2 * d, d, q, span(e)], taken.at[d, d, q, span(e)], x_s.at[d, kind, q], x_r.at[d, kind, q], beyond(d)
        )

    def z_home(m, c, e=None):
        sem = step_of(c, e)
        return remote(leaving.at[0, m, c, span(e)], landed.at[0, m, c, span(e)], z_s.at[0, m, sem], z_r.at[0, m, sem], beside)

    def step_of(c, e):
        return c if e is None else c + e

    def z_add(c, e=None):
        sem, at = step_of(c, e), span(e)
        return remote(leaving.at[1, 0, c, at], landed.at[1, 0, c, at], z_s.at[1, 0, sem], z_r.at[1, 0, sem], beside)

    def z_on(m, c, e=None):
        sem, at = step_of(c, e), span(e)
        return remote(leaving.at[1, m, c, at], landed.at[0, m, c, at], z_s.at[1, m, sem], z_r.at[0, m, sem], corner)

    def z_via(c, e=None):
        sem, at = step_of(c, e), span(e)
        return remote(leaving.at[1, 1, c, at], passing.at[c, at], z_s.at[1, 1, sem], z_r.at[1, 1, sem], corner)

    def z_fwd(c, e=None):
        sem, at = step_of(c, e), span(e)
        return remote(passing.at[c, at], landed.at[1, 1, c, at], z_fs.at[sem], z_fr.at[sem], beside)

    def rhs_to(step):
        peer = (p, (o + step) % 16)
        return remote(rhs_all.at[o], rhs_all.at[o], rhs_s.at[step], rhs_r.at[step], peer)

    incoming = pltpu.make_async_copy(design_hbm, design, design_s)
    incoming.start()

    barrier = pltpu.get_barrier_semaphore()
    greeted = [(param_of(y + step, h), obs_of(x, l, core)) for step in (1, -1) for core in (k, 1 - k)] + [across, corner]
    greeted += [(p, (o + step) % 16) for step in range(1, 16)]
    for device in greeted:
        pl.semaphore_signal(barrier, inc=1, device_id=device, device_id_type=MESH)

    signal_row = jnp.broadcast_to(observed[...].astype(F32).reshape(1, ROWS), (8, ROWS))
    weight_row = jnp.broadcast_to(weight[...].reshape(1, ROWS), (8, ROWS))
    obs_tail[...] = signal_row[:, ROWS - 128 :]
    for r in range(ROWS // 128):
        block = jnp.broadcast_to(weight_row[0:1, r * 128 : (r + 1) * 128], (128, 128))
        wcol[pl.ds(r * 128, 128), :] = block.T

    def order(i):
        return i // 4, i % 2, 1 - (i // 2) % 2

    def filter_rows(i, r):
        e, m, rel = order(i)
        core = (k + rel) % 2
        at = pl.ds(pl.multiple_of(core * 512 + m * PART + e * 128, 128), 128)
        quarter = pl.ds(pl.multiple_of((core * 2 + m) * 128, 128), 128)
        first = r * 128
        total = ext[pl.ds(8 + first, 128), at]
        for lag in range(1, LAGS + 1):
            total = total + taps[lag - 1] * ext[pl.ds(8 + first - lag, 128), at]
        rounded = total.astype(BF16).astype(F32)
        cols[0, e, pl.ds(first, 128), quarter] = (wcol[pl.ds(first, 128), :] * rounded).astype(BF16)
        turned = rounded.T.astype(BF16)
        mine[rel, m, span(e), pl.ds(first, 128)] = turned

        @pl.when(rel == 0)
        def _():
            rows[0, m, span(e), pl.ds(first, 128)] = turned

    def filter_later_rows(i, _):
        e, m, rel = order(i)
        at = pl.ds(pl.multiple_of((k + rel) % 2 * 512 + m * PART + e * 128, 128), 128)
        ext[pl.ds(8, ROWS), at] = design[:, at].astype(F32)
        for r in range(1, ROWS // 128):
            filter_rows(i, r)
        return 0

    incoming.wait()
    lax.fori_loop(0, 2, filter_later_rows, 0)
    pl.semaphore_wait(barrier, len(greeted))

    @pl.when(o < 15)
    def _():
        for copy in halo_copies():
            copy.start()

    def start_early(i, _):
        e, m, rel = order(i)
        rows_out(m, rel, 0, 1 - m, 128).start()
        return 0

    def filter_and_start(i, _):
        filter_later_rows(i, _)
        return start_early(i, _)

    lax.fori_loop(0, 2, start_early, 0)
    lax.fori_loop(2, 4, filter_and_start, 0)
    cols_across(0, 128).start()
    cols_over(0, 128).start()
    lax.fori_loop(4, 8, filter_later_rows, 0)

    @pl.when(o > 0)
    def _():
        for copy in halo_copies():
            copy.wait_recv()
        ext[pl.ds(0, 8), :] = halo[...].astype(F32)[8:]

    @pl.when(o == 0)
    def _():
        ext[pl.ds(0, 8), :] = jnp.zeros((8, COLS), F32)
        obs_halo[...] = jnp.zeros((8, 128), F32)

    def first_pieces():
        return [rows_out(m, rel, e, 1 - m) for e in range(2) for m in range(2) for rel in (1, 0)]

    def second_pieces():
        return [rows_out(m, rel, e, m) for e in range(2) for m in range(2) for rel in (1, 0)]

    def passed_on(halves=(0, 1)):
        return [rows_on(m, rel, e) for e in halves for m in range(2) for rel in (1, 0)]

    def arrived(dy, m):
        for rel in (1, 0):
            for e in range(2):
                rows_at(dy, m, rel, e).wait_recv()

    def filter_block(i, _):
        e, m, rel = order(i)
        filter_rows(i, 0)

        @pl.when(e == 0)
        def _():
            rows_out(m, rel, e, 1 - m, 0, 128).start()

        @pl.when(e == 1)
        def _():
            rows_out(m, rel, e, 1 - m).start()

        @pl.when(rel == 1)
        def _():
            rows_over(m, e).start()

        @pl.when(i == 3)
        def _():
            cols_across(0, 0, 128).start()
            cols_over(0, 0, 128).start()

        return 0

    lax.fori_loop(0, 8, filter_block, 0)
    cols_across(1).start()
    cols_over(1).start()
    first_far = near == 2

    @pl.when(first_far)
    def _():
        for copy in second_pieces():
            copy.start()

    def multiply(dy, m, q, e=None):
        role = (near + dy) % 4

        def chunk(c, _):
            at = pl.ds(pl.multiple_of(c * 256, 256), 256)
            value = jnp.dot(rows[dy, m, span(e)], cols[q // 2, q % 2, :, at], preferred_element_type=F32)

            @pl.when(role == 0)
            def _():
                own[m, q, span(e), at] = value

            @pl.when(role != 0)
            def _():
                part[role - 1, m, q, span(e), at] = value.astype(BF16)

            return 0

        lax.fori_loop(0, 2, chunk, 0)

        @pl.when(role == 2)
        def _():
            x_far(m, q, e).start()

        @pl.when(jnp.logical_or(jnp.logical_and(role == 1, m == 1), jnp.logical_and(role == 3, m == 0)))
        def _():
            x_raw(role // 2, q, e).start()

    def add_far(d, q, valid=True, halves=None):
        @pl.when(valid)
        def _():
            if halves is None or 0 in halves:
                x_far(d, q).wait_recv()
            for e in halves_of(q) if halves is None else halves:
                both = part[2 * d, d, q, span(e)].astype(F32) + far[d, q, span(e)].astype(F32)
                part[2 * d, d, q, span(e)] = both.astype(BF16)
                x_sum(d, q, e).start()

    def halves_of(q):
        return (0, 1) if isinstance(q, int) and q % 2 == 1 else (None,)

    def by_near(*values):
        chosen = values[3]
        for place in (2, 1, 0):
            chosen = jnp.where(near == place, values[place], chosen)
        return chosen

    for m in range(2):
        for e in range(2):
            rows_over(m, e).wait_recv()
        cols_over(m).wait_recv()
    for q in range(2):
        for m in (1, 0):
            multiply(0, m, q)

    for e in range(2):
        for m in range(2):
            for rel in (1, 0):
                rows_at(3 - 2 * m, m, rel, e).wait_recv()
        for copy in passed_on((e,)):
            copy.start()
        if e == 1:

            @pl.when(jnp.logical_not(first_far))
            def _():
                for copy in second_pieces():
                    copy.start()

        for q in range(2):
            multiply(3, 0, q, e)
            multiply(1, 1, q, e)
        add_far(by_near(0, 0, 0, 1), e, (near % 2) == 1)
    cols_across(0).wait_recv()
    cols_on(0).start()
    cols_on(0).wait_recv()
    multiply(by_near(3, 0, 0, 0), by_near(0, 1, 1, 1), 2)
    multiply(by_near(1, 0, 0, 0), by_near(1, 0, 0, 0), 2)
    multiply(by_near(0, 3, 3, 3), by_near(1, 0, 0, 0), 2)
    multiply(by_near(0, 1, 1, 1), by_near(0, 1, 1, 1), 2)
    for q in range(2):
        for d in range(2):
            add_far(d, q, near == 2)

    extended = jnp.concatenate([obs_halo[...], signal_row], axis=1)
    total = signal_row
    for lag in range(1, LAGS + 1):
        total = total + taps[lag - 1] * pltpu.roll(extended, lag, 1)[:, 128:]
    filtered_obs[...] = total[0:1, :].reshape(ROWS)
    weighted[...] = jnp.concatenate([weight_row * total, weight_row * total], axis=0).astype(BF16)
    line = lax.broadcasted_iota(jnp.int32, (8, 128), 0)
    sums = jnp.zeros((8, 128), F32)
    for m in range(2):
        for rel in range(2):
            core = (k + rel) % 2
            dots = lax.dot_general(weighted[...], mine[rel, m], (((1,), (1,)), ((), ())), preferred_element_type=F32)
            for c in range(2):
                sums = jnp.where(line == core * 4 + m * 2 + c, dots[0:8, c * 128 : (c + 1) * 128], sums)
    rhs_all[o] = sums
    for step in range(1, 16):
        rhs_to(step).start()

    third = (by_near(2, 1, 2, 3), by_near(0, 0, 0, 1))
    fourth = (2, by_near(1, 0, 1, 1))
    fifth = (by_near(1, 2, 1, 2), by_near(0, 1, 0, 0))
    sixth = (by_near(3, 3, 3, 1), by_near(1, 1, 1, 0))
    arrived(*third)
    multiply(*third, 0)
    arrived(*fourth)
    multiply(*fourth, 0)
    multiply(*third, 2)
    multiply(*fourth, 2)
    cols_across(1).wait_recv()
    cols_on(1).start()
    cols_on(1).wait_recv()

    def last_sums(q, valid=True, halves=None):
        add_far(by_near(0, 1, 0, 0), q, valid, halves)
        add_far(1, q, jnp.logical_and(valid, (near % 2) == 0), halves)

    multiply(by_near(2, 1, 0, 3), by_near(0, 0, 1, 1), 3)
    multiply(by_near(2, 1, 0, 3), by_near(1, 1, 0, 0), 3)

    @pl.when(near != 0)
    def _():
        multiply(*third, 1)

    add_far(by_near(0, 0, 0, 1), 2, near != 0)
    add_far(1, 2, near == 2)
    multiply(by_near(3, 0, 3, 0), by_near(0, 0, 0, 1), 3)
    multiply(by_near(1, 0, 1, 0), by_near(1, 1, 1, 0), 3)

    for piece in (fifth, sixth):
        arrived(*piece)
    for q in (0, 2):
        for piece in (fifth, sixth):
            multiply(*piece, q)
        last_sums(q, near != 2)

    @pl.when(near == 0)
    def _():
        multiply(*third, 1)

    multiply(*fourth, 1)
    multiply(by_near(0, 2, 2, 2), by_near(0, 0, 0, 1), 3)
    multiply(by_near(0, 3, 2, 1), by_near(1, 0, 1, 1), 3)
    add_far(by_near(0, 0, 0, 1), 3, (near % 2) == 1)
    for piece in (fifth, sixth):
        multiply(*piece, 3)
    last_sums(3, near == 2)
    last_sums(3, near != 2, (0,))
    for piece in (fifth, sixth):
        multiply(*piece, 1)

    def final_sums(valid):
        last_sums(1, valid, (0,))
        last_sums(3, valid, (1,))
        last_sums(1, valid, (1,))

    final_sums(near == 0)

    for step in range(1, 16):
        rhs_to(step).wait_recv()
    total = rhs_all[0]
    for step in range(1, 16):
        total = total + rhs_all[step]
    rhs[...] = (total * rhs_scale).reshape(COLS)

    def summed(m, q, e=None):
        x_sum(m, q, e).wait_recv()
        if not e:
            x_raw(1 - m, q).wait_recv()
        return own[m, q, span(e)] + taken[0, m, q, span(e)].astype(F32) + taken[1, m, q, span(e)].astype(F32)

    def keep_near(c, e=None):
        for m in range(2):
            total = summed(m, c, e)

            @pl.when(settled)
            def _():
                own[m, c, span(e)] = total

            @pl.when(jnp.logical_not(settled))
            def _():
                leaving[0, m, c, span(e)] = total.astype(BF16)
                z_home(m, c, e).start()

    def pass_over(c, e=None):
        for m in (1, 0):
            total = summed(m, 2 + c, e)

            @pl.when(settled)
            def _():
                leaving[1, m, c, span(e)] = total.astype(BF16)
                (z_add(c, e) if m == 0 else z_via(c, e)).start()

            @pl.when(jnp.logical_not(settled))
            def _():
                if m == 0:
                    own[m, 2 + c, span(e)] = total
                else:
                    leaving[1, m, c, span(e)] = total.astype(BF16)
                    z_on(m, c, e).start()

    def pass_on(c, e=None):
        @pl.when(settled)
        def _():
            z_via(c, e).wait_recv()
            z_fwd(c, e).start()

        @pl.when(jnp.logical_not(settled))
        def _():
            z_add(c, e).wait_recv()
            leaving[1, 0, c, span(e)] = (own[0, 2 + c, span(e)] + landed[1, 0, c, span(e)].astype(F32)).astype(BF16)
            z_on(0, c, e).start()

    keep_near(0)
    pass_over(0)
    final_sums((near % 2) == 1)
    pass_on(0)
    pass_over(1, 0)
    keep_near(1, 0)
    pass_on(1, 0)
    pass_over(1, 1)
    keep_near(1, 1)
    pass_on(1, 1)

    def place(m, c, total):
        for b in range(4):
            to = pl.ds(b // 2 * 512 + b % 2 * 256 + c * 128, 128)
            normal[pl.ds(m * PART, PART), to] = total[:, b * 128 : b * 128 + 128] * scale

    for c in range(2):
        for m in range(2):

            @pl.when(settled)
            def _():
                for e in halves_of(c):
                    z_home(m, c, e).wait_recv()
                place(m, c, own[m, c] + landed[0, m, c].astype(F32))

            @pl.when(jnp.logical_not(settled))
            def _():
                for e in halves_of(c):
                    z_on(m, c, e).wait_recv()
                total = landed[0, m, c].astype(F32)
                if m == 1:
                    for e in halves_of(c):
                        z_fwd(c, e).wait_recv()
                    total = total + landed[1, 1, c].astype(F32)
                place(m, c, total)

    @pl.when(o < 15)
    def _():
        for copy in halo_copies():
            copy.wait_send()

    for m in range(2):
        for e in range(2):
            rows_over(m, e).wait_send()
        cols_over(m).wait_send()
        cols_across(m).wait_send()
        cols_on(m).wait_send()
        for c in range(2):
            for e in halves_of(c):
                z_on(m, c, e).wait_send()

            @pl.when(jnp.logical_not(settled))
            def _():
                for e in halves_of(c):
                    z_home(m, c, e).wait_send()

        @pl.when(settled)
        def _():
            for e in halves_of(m):
                z_fwd(m, e).wait_send()

        for q in range(4):
            x_far(m, q).wait_send()
            x_raw(m, q).wait_send()
            for e in halves_of(q):
                x_sum(m, q, e).wait_send()
    for copy in first_pieces() + passed_on() + second_pieces():
        copy.wait_send()
    for step in range(1, 16):
        rhs_to(step).wait_send()


def per_device(design, observed, row_weight, taps):
    total_rows = ROWS * lax.axis_size("obs")
    dma = pltpu.SemaphoreType.DMA
    vmem = pl.BlockSpec(memory_space=pltpu.VMEM)
    normal, rhs, filtered_obs = pl.pallas_call(
        functools.partial(kernel, 1.0 / total_rows, 1.0 / math.sqrt(total_rows)),
        out_shape=(
            jax.ShapeDtypeStruct((512, COLS), F32),
            jax.ShapeDtypeStruct((COLS,), F32),
            jax.ShapeDtypeStruct((ROWS,), F32),
        ),
        in_specs=[pl.BlockSpec(memory_space=pl.ANY), vmem, vmem, pl.BlockSpec(memory_space=pltpu.SMEM)],
        out_specs=(vmem, vmem, vmem),
        scratch_shapes=[
            pltpu.VMEM((ROWS, COLS), BF16),
            pltpu.VMEM((ROWS + 8, COLS), F32),
            pltpu.VMEM((16, COLS), BF16),
            pltpu.VMEM((8, 128), F32),
            pltpu.VMEM((8, 128), F32),
            pltpu.VMEM((ROWS, 128), F32),
            pltpu.VMEM((2, 2, PART, ROWS), BF16),
            pltpu.VMEM((16, ROWS), BF16),
            pltpu.VMEM((4, 2, PART, DEPTH), BF16),
            pltpu.VMEM((2, 2, DEPTH, 512), BF16),
            pltpu.VMEM((3, 2, 4, PART, 512), BF16),
            pltpu.VMEM((2, 4, PART, 512), F32),
            pltpu.VMEM((2, 2, 4, PART, 512), BF16),
            pltpu.VMEM((2, 4, PART, 512), BF16),
            pltpu.VMEM((2, 2, 2, PART, 512), BF16),
            pltpu.VMEM((2, 2, 2, PART, 512), BF16),
            pltpu.VMEM((2, PART, 512), BF16),
            pltpu.VMEM((16, 8, 128), F32),
            dma, dma((2,)), dma((2,)),
            dma((2, 2, 2, 2)), dma((2, 2, 2)), dma((2, 2)), dma((4, 2, 2, 2)),
            dma((2,)), dma((2,)), dma((2,)), dma((2, 2, 2)),
            dma((2, 4, 4)), dma((2, 4, 4)),
            dma((2, 2, 3)), dma((2, 2, 3)), dma((3,)), dma((3,)),
            dma((16,)), dma((16,)),
        ],
        compiler_params=pltpu.CompilerParams(collective_id=0, has_side_effects=True, vmem_limit_bytes=60 << 20),
        name="normal_equations",
    )(design, observed, row_weight, taps)
    return normal, rhs, filtered_obs


def solution(mesh):
    placed = (P("obs", "param"), P("obs"), P("obs"), P())
    return jax.shard_map(
        per_device,
        mesh=mesh,
        in_specs=placed,
        out_specs=(P("obs", "param"), P("param"), P("obs")),
        check_vma=False,
    )
```

```python
import functools
import math

import jax
import jax.numpy as jnp
from jax import lax
from jax.experimental import pallas as pl
from jax.experimental.pallas import tpu as pltpu
from jax.sharding import PartitionSpec as P

MESH = pl.DeviceIdType.MESH
BF16, F32 = jnp.bfloat16, jnp.float32
ROWS = 640
COLS = 1024
LAGS = 7
PART = 256
DEPTH = 2 * ROWS


def kernel(
    scale, rhs_scale,
    design_hbm, observed, weight, taps,
    normal, rhs, filtered_obs,
    design, ext, halo, obs_tail, obs_halo, wcol, mine, weighted, rows, cols, part, own, taken, far, giving, swapped,
    leaving, landed, passing, rhs_all,
    design_s, halo_s, halo_r, rows_s, rows_f, rows_sib, rows_r, cols_s, cols_sib, cols_f, cols_r, x_s, x_r, swap_s, swap_r, z_s, z_r, z_fs, z_fr, rhs_s, rhs_r,
):
    p, o = lax.axis_index("param"), lax.axis_index("obs")
    y, h = p // 2, p % 2
    x, l, k = o // 4, (o // 2) % 2, o % 2
    near = (y - x + 4) % 4
    settled = l == h
    kept, given = jnp.where(settled, 1, 3), jnp.where(settled, 3, 1)

    def param_of(y_, h_):
        return ((y_ + 4) % 4) * 2 + h_

    def obs_of(x_, l_, k_):
        return ((x_ + 4) % 4) * 4 + l_ * 2 + k_

    sibling = (p, obs_of(x, l, 1 - k))
    across = (param_of(y, 1 - h), o)
    beside = (p, obs_of(x, 1 - l, k))
    corner = (param_of(y, 1 - h), obs_of(x, 1 - l, k))
    following = (p, (o + 1) % 16)

    def remote(src, dst, send, recv, device):
        return pltpu.make_async_remote_copy(
            src_ref=src, dst_ref=dst, send_sem=send, recv_sem=recv, device_id=device, device_id_type=MESH
        )

    def halo_copies():
        return (
            remote(design.at[pl.ds(ROWS - 16, 16), :], halo, halo_s.at[0], halo_r.at[0], following),
            remote(obs_tail, obs_halo, halo_s.at[1], halo_r.at[1], following),
        )

    def lanes(rel):
        return pl.ds(ROWS * rel, ROWS)

    def span(e):
        return pl.ds(0, PART) if e is None else pl.ds(pl.multiple_of(e * 128, 128), 128)

    def wide(c):
        return pl.ds(c * 512, 512)

    def rows_out(m, rel, e, up, begin=0, end=ROWS):
        target = (param_of(y + 2 * up - 1, h), obs_of(x, l, (k + rel) % 2))
        dy = 1 + 2 * up
        to = pl.ds(pl.multiple_of(ROWS * rel + begin, 128), end - begin)
        return remote(
            mine.at[rel, m, span(e), pl.ds(begin, end - begin)], rows.at[dy, m, span(e), to],
            rows_s.at[up, m, rel, e], rows_r.at[dy, m, rel, e], target,
        )

    def rows_on(m, rel, e):
        target = (param_of(y + 1 - 2 * m, h), o)
        return remote(
            rows.at[3 - 2 * m, m, span(e), lanes(rel)], rows.at[2, m, span(e), lanes(rel)],
            rows_f.at[m, rel, e], rows_r.at[2, m, rel, e], target,
        )

    def rows_at(dy, m, rel, e):
        piece = rows.at[dy, m, span(e), lanes(rel)]
        return remote(piece, piece, rows_f.at[0, 0, 0], rows_r.at[dy, m, rel, e], following)

    def rows_over(m, e):
        return remote(mine.at[1, m, span(e)], rows.at[0, m, span(e), lanes(1)], rows_sib.at[m, e], rows_r.at[0, m, 1, e], sibling)

    def cols_over(n, begin=0, end=ROWS):
        half, other = pl.ds(begin, end - begin), pl.ds(ROWS + begin, end - begin)
        return remote(cols.at[0, n, half, :], cols.at[0, n, other, :], cols_sib.at[n], cols_r.at[0, n, 1], sibling)

    def cols_across(n, begin=0, end=ROWS):
        half = pl.ds(begin, end - begin)
        return remote(cols.at[0, n, half, :], cols.at[1, n, half, :], cols_s.at[n], cols_r.at[1, n, 0], across)

    def cols_on(n):
        half = pl.ds(0, ROWS)
        return remote(cols.at[1, n, half, :], cols.at[1, n, pl.ds(ROWS, ROWS), :], cols_f.at[n], cols_r.at[1, n, 1], sibling)

    def beyond(d):
        return (p, obs_of(x + 1 - 2 * d, l, k))

    def x_far(d, q, e=None, late=0):
        at = span(e)
        return remote(part.at[1, d, q, at], far.at[d, q, at], x_s.at[d, 3 * late, q], x_r.at[d, 3 * late, q], beyond(d))

    def x_raw(d, q, e=None, late=0):
        at, kind = span(e), 1 + 3 * late
        dst = taken.at[d, 1 - d, q, at]
        return remote(part.at[2 * d, 1 - d, q, at], dst, x_s.at[d, kind, q], x_r.at[d, kind, q], beyond(d))

    def x_sum(d, q, e=None, late=0):
        at, kind = span(e), 2 + 3 * late
        return remote(part.at[2 * d, d, q, at], taken.at[d, d, q, at], x_s.at[d, kind, q], x_r.at[d, kind, q], beyond(d))

    def swap(role, m):
        place = part.at[role - 1, m, given, span(1)]
        return remote(place, swapped.at[role, m], swap_s.at[role, m], swap_r.at[role, m], beside)

    def swap_own(m):
        return remote(giving.at[m], swapped.at[0, m], swap_s.at[0, m], swap_r.at[0, m], beside)

    def z_home(m, c, e=None):
        sem = step_of(c, e)
        return remote(leaving.at[0, m, c, span(e)], landed.at[0, m, c, span(e)], z_s.at[0, m, sem], z_r.at[0, m, sem], beside)

    def step_of(c, e):
        return c if e is None else c + e

    def z_add(c, e=None):
        sem, at = step_of(c, e), span(e)
        return remote(leaving.at[1, 0, c, at], landed.at[1, 0, c, at], z_s.at[1, 0, sem], z_r.at[1, 0, sem], beside)

    def z_on(m, c, e=None):
        sem, at = step_of(c, e), span(e)
        return remote(leaving.at[1, m, c, at], landed.at[0, m, c, at], z_s.at[1, m, sem], z_r.at[0, m, sem], corner)

    def z_via(c, e=None):
        sem, at = step_of(c, e), span(e)
        return remote(leaving.at[1, 1, c, at], passing.at[c, at], z_s.at[1, 1, sem], z_r.at[1, 1, sem], corner)

    def z_fwd(c, e=None):
        sem, at = step_of(c, e), span(e)
        return remote(passing.at[c, at], landed.at[1, 1, c, at], z_fs.at[sem], z_fr.at[sem], beside)

    def rhs_to(step):
        peer = (p, (o + step) % 16)
        return remote(rhs_all.at[o], rhs_all.at[o], rhs_s.at[step], rhs_r.at[step], peer)

    incoming = pltpu.make_async_copy(design_hbm, design, design_s)
    incoming.start()

    barrier = pltpu.get_barrier_semaphore()
    greeted = [(param_of(y + step, h), obs_of(x, l, core)) for step in (1, -1) for core in (k, 1 - k)] + [across, corner]
    greeted += [(p, (o + step) % 16) for step in range(1, 16)]
    for device in greeted:
        pl.semaphore_signal(barrier, inc=1, device_id=device, device_id_type=MESH)

    signal_row = jnp.broadcast_to(observed[...].astype(F32).reshape(1, ROWS), (8, ROWS))
    weight_row = jnp.broadcast_to(weight[...].reshape(1, ROWS), (8, ROWS))
    obs_tail[...] = signal_row[:, ROWS - 128 :]
    for r in range(ROWS // 128):
        block = jnp.broadcast_to(weight_row[0:1, r * 128 : (r + 1) * 128], (128, 128))
        wcol[pl.ds(r * 128, 128), :] = block.T

    def order(i):
        return i // 4, i % 2, 1 - (i // 2) % 2

    def filter_rows(i, r):
        e, m, rel = order(i)
        core = (k + rel) % 2
        at = pl.ds(pl.multiple_of(core * 512 + m * PART + e * 128, 128), 128)
        quarter = pl.ds(pl.multiple_of((core * 2 + m) * 128, 128), 128)
        first = r * 128
        total = ext[pl.ds(8 + first, 128), at]
        for lag in range(1, LAGS + 1):
            total = total + taps[lag - 1] * ext[pl.ds(8 + first - lag, 128), at]
        rounded = total.astype(BF16).astype(F32)
        cols[0, e, pl.ds(first, 128), quarter] = (wcol[pl.ds(first, 128), :] * rounded).astype(BF16)
        turned = rounded.T.astype(BF16)
        mine[rel, m, span(e), pl.ds(first, 128)] = turned

        @pl.when(rel == 0)
        def _():
            rows[0, m, span(e), pl.ds(first, 128)] = turned

    def filter_later_rows(i, _):
        e, m, rel = order(i)
        at = pl.ds(pl.multiple_of((k + rel) % 2 * 512 + m * PART + e * 128, 128), 128)
        ext[pl.ds(8, ROWS), at] = design[:, at].astype(F32)
        for r in range(1, ROWS // 128):
            filter_rows(i, r)
        return 0

    incoming.wait()
    lax.fori_loop(0, 2, filter_later_rows, 0)
    pl.semaphore_wait(barrier, len(greeted))

    @pl.when(o < 15)
    def _():
        for copy in halo_copies():
            copy.start()

    def start_early(i, _):
        e, m, rel = order(i)
        rows_out(m, rel, 0, 1 - m, 128).start()
        return 0

    def filter_and_start(i, _):
        filter_later_rows(i, _)
        return start_early(i, _)

    lax.fori_loop(0, 2, start_early, 0)
    lax.fori_loop(2, 4, filter_and_start, 0)
    cols_across(0, 128).start()
    cols_over(0, 128).start()
    lax.fori_loop(4, 8, filter_later_rows, 0)

    @pl.when(o > 0)
    def _():
        for copy in halo_copies():
            copy.wait_recv()
        ext[pl.ds(0, 8), :] = halo[...].astype(F32)[8:]

    @pl.when(o == 0)
    def _():
        ext[pl.ds(0, 8), :] = jnp.zeros((8, COLS), F32)
        obs_halo[...] = jnp.zeros((8, 128), F32)

    def first_pieces():
        return [rows_out(m, rel, e, 1 - m) for e in range(2) for m in range(2) for rel in (1, 0)]

    def second_pieces():
        return [rows_out(m, rel, e, m) for e in range(2) for m in range(2) for rel in (1, 0)]

    def passed_on(halves=(0, 1)):
        return [rows_on(m, rel, e) for e in halves for m in range(2) for rel in (1, 0)]

    def arrived(dy, m):
        for rel in (1, 0):
            for e in range(2):
                rows_at(dy, m, rel, e).wait_recv()

    def filter_block(i, _):
        e, m, rel = order(i)
        filter_rows(i, 0)

        @pl.when(e == 0)
        def _():
            rows_out(m, rel, e, 1 - m, 0, 128).start()

        @pl.when(e == 1)
        def _():
            rows_out(m, rel, e, 1 - m).start()

        @pl.when(rel == 1)
        def _():
            rows_over(m, e).start()

        @pl.when(i == 3)
        def _():
            cols_across(0, 0, 128).start()
            cols_over(0, 0, 128).start()

        return 0

    lax.fori_loop(0, 8, filter_block, 0)
    cols_across(1).start()
    cols_over(1).start()
    first_far = near == 2

    @pl.when(first_far)
    def _():
        for copy in second_pieces():
            copy.start()

    def multiply(dy, m, q, e=None):
        role = (near + dy) % 4

        def chunk(c, _):
            at = pl.ds(pl.multiple_of(c * 256, 256), 256)
            value = jnp.dot(rows[dy, m, span(e)], cols[q // 2, q % 2, :, at], preferred_element_type=F32)

            @pl.when(role == 0)
            def _():
                own[m, q, span(e), at] = value

            @pl.when(role != 0)
            def _():
                part[role - 1, m, q, span(e), at] = value.astype(BF16)

            return 0

        lax.fori_loop(0, 2, chunk, 0)

        if q % 2 == 1 and e == 1:
            return
        e = 0 if q % 2 == 1 else e

        @pl.when(role == 2)
        def _():
            x_far(m, q, e).start()

        @pl.when(as_it_is(role, m))
        def _():
            x_raw(role // 2, q, e).start()

    def as_it_is(role, m):
        return jnp.logical_or(jnp.logical_and(role == 1, m == 1), jnp.logical_and(role == 3, m == 0))

    def give(dy, m):
        role = (near + dy) % 4

        @pl.when(role == 0)
        def _():
            giving[m] = own[m, given, span(1)].astype(BF16)
            swap_own(m).start()

        @pl.when(role != 0)
        def _():
            swap(role, m).start()

    def take(dy, m):
        role = (near + dy) % 4

        @pl.when(role == 0)
        def _():
            swap_own(m).wait_recv()
            own[m, kept, span(1)] = own[m, kept, span(1)] + swapped[0, m].astype(F32)

        @pl.when(role != 0)
        def _():
            swap(role, m).wait_recv()
            both = part[role - 1, m, kept, span(1)].astype(F32) + swapped[role, m].astype(F32)
            part[role - 1, m, kept, span(1)] = both.astype(BF16)

        @pl.when(role == 2)
        def _():
            x_far(m, kept, 1, 1).start()

        @pl.when(as_it_is(role, m))
        def _():
            x_raw(role // 2, kept, 1, 1).start()

    def add_far(d, q, valid=True, late=0):
        e = late if late else first_of(q)

        @pl.when(valid)
        def _():
            x_far(d, q, e, late).wait_recv()
            both = part[2 * d, d, q, span(e)].astype(F32) + far[d, q, span(e)].astype(F32)
            part[2 * d, d, q, span(e)] = both.astype(BF16)
            x_sum(d, q, e, late).start()

    def first_of(q):
        return 0 if q % 2 == 1 else None

    def by_near(*values):
        chosen = values[3]
        for place in (2, 1, 0):
            chosen = jnp.where(near == place, values[place], chosen)
        return chosen

    for m in range(2):
        for e in range(2):
            rows_over(m, e).wait_recv()
        cols_over(m).wait_recv()
    for q in range(2):
        for m in (1, 0):
            multiply(0, m, q)

    for e in range(2):
        for m in range(2):
            for rel in (1, 0):
                rows_at(3 - 2 * m, m, rel, e).wait_recv()
        for copy in passed_on((e,)):
            copy.start()
        if e == 1:

            @pl.when(jnp.logical_not(first_far))
            def _():
                for copy in second_pieces():
                    copy.start()

        for q in range(2):
            multiply(3, 0, q, e)
            multiply(1, 1, q, e)
        add_far(by_near(0, 0, 0, 1), e, (near % 2) == 1)
    cols_across(0).wait_recv()
    cols_on(0).start()
    cols_on(0).wait_recv()
    multiply(by_near(3, 0, 0, 0), by_near(0, 1, 1, 1), 2)
    multiply(by_near(1, 0, 0, 0), by_near(1, 0, 0, 0), 2)
    multiply(by_near(0, 3, 3, 3), by_near(1, 0, 0, 0), 2)
    multiply(by_near(0, 1, 1, 1), by_near(0, 1, 1, 1), 2)
    for q in range(2):
        for d in range(2):
            add_far(d, q, near == 2)

    extended = jnp.concatenate([obs_halo[...], signal_row], axis=1)
    total = signal_row
    for lag in range(1, LAGS + 1):
        total = total + taps[lag - 1] * pltpu.roll(extended, lag, 1)[:, 128:]
    filtered_obs[...] = total[0:1, :].reshape(ROWS)
    weighted[...] = jnp.concatenate([weight_row * total, weight_row * total], axis=0).astype(BF16)
    line = lax.broadcasted_iota(jnp.int32, (8, 128), 0)
    sums = jnp.zeros((8, 128), F32)
    for m in range(2):
        for rel in range(2):
            core = (k + rel) % 2
            dots = lax.dot_general(weighted[...], mine[rel, m], (((1,), (1,)), ((), ())), preferred_element_type=F32)
            for c in range(2):
                sums = jnp.where(line == core * 4 + m * 2 + c, dots[0:8, c * 128 : (c + 1) * 128], sums)
    rhs_all[o] = sums
    for step in range(1, 16):
        rhs_to(step).start()

    third = (by_near(2, 1, 2, 3), by_near(0, 0, 0, 1))
    fourth = (2, by_near(1, 0, 1, 1))
    fifth = (by_near(1, 2, 1, 2), by_near(0, 1, 0, 0))
    sixth = (by_near(3, 3, 3, 1), by_near(1, 1, 1, 0))
    arrived(*third)
    multiply(*third, 2)
    arrived(*fourth)
    multiply(*fourth, 2)
    for q in (0, 1):
        multiply(*third, q)
        multiply(*fourth, q)
    cols_across(1).wait_recv()
    cols_on(1).start()
    cols_on(1).wait_recv()

    def last_sums(q, valid=True):
        add_far(by_near(0, 1, 0, 0), q, valid)
        add_far(1, q, jnp.logical_and(valid, (near % 2) == 0))

    slots = (
        (by_near(2, 1, 0, 3), by_near(0, 0, 1, 1)),
        (by_near(2, 1, 0, 3), by_near(1, 1, 0, 0)),
        (by_near(3, 0, 3, 0), by_near(0, 0, 0, 1)),
        (by_near(1, 0, 1, 0), by_near(1, 1, 1, 0)),
        (by_near(0, 2, 2, 2), by_near(0, 0, 0, 1)),
        (by_near(0, 3, 2, 1), by_near(1, 0, 1, 1)),
    )
    def summed(m, q, e=None, late=0):
        x_sum(m, q, e, late).wait_recv()
        x_raw(1 - m, q, e, late).wait_recv()
        return own[m, q, span(e)] + taken[0, m, q, span(e)].astype(F32) + taken[1, m, q, span(e)].astype(F32)

    def keep_near(c, e=None):
        for m in range(2):
            total = summed(m, c, e)

            @pl.when(settled)
            def _():
                own[m, c, span(e)] = total

            @pl.when(jnp.logical_not(settled))
            def _():
                leaving[0, m, c, span(e)] = total.astype(BF16)
                z_home(m, c, e).start()

    def pass_over(c, e=None):
        for m in (1, 0):
            total = summed(m, 2 + c, e)

            @pl.when(settled)
            def _():
                leaving[1, m, c, span(e)] = total.astype(BF16)
                (z_add(c, e) if m == 0 else z_via(c, e)).start()

            @pl.when(jnp.logical_not(settled))
            def _():
                if m == 0:
                    own[m, 2 + c, span(e)] = total
                else:
                    leaving[1, m, c, span(e)] = total.astype(BF16)
                    z_on(m, c, e).start()

    def hand_on(c, e=None):
        @pl.when(settled)
        def _():
            z_via(c, e).wait_recv()
            z_fwd(c, e).start()

    def add_on(c, e=None):
        @pl.when(jnp.logical_not(settled))
        def _():
            z_add(c, e).wait_recv()
            leaving[1, 0, c, span(e)] = (own[0, 2 + c, span(e)] + landed[1, 0, c, span(e)].astype(F32)).astype(BF16)
            z_on(0, c, e).start()

    def late_sums(valid):
        for d in range(2):
            add_far(d, kept, valid, 1)

    for slot in slots[0:2]:
        multiply(*slot, 3)
        give(*slot)
    add_far(by_near(0, 0, 0, 1), 2, near != 0)
    add_far(1, 2, near == 2)
    for slot in slots[2:6]:
        multiply(*slot, 3)
        give(*slot)
    for piece in (fifth, sixth):
        arrived(*piece)
    for piece in (fifth, sixth):
        multiply(*piece, 2)
    last_sums(2, near != 2)
    for slot in slots[0:2]:
        take(*slot)
    for piece in (fifth, sixth):
        multiply(*piece, 0)
    last_sums(0, near != 2)
    add_far(by_near(0, 0, 0, 1), 3, (near % 2) == 1)
    for piece in (fifth, sixth):
        multiply(*piece, 3)
        multiply(*piece, 1)
        give(*piece)
    for slot in slots[2:4]:
        take(*slot)
    last_sums(3)
    last_sums(1, near == 0)

    @pl.when(near == 0)
    def _():
        pass_over(0)

    for slot in slots[4:6] + (fifth, sixth):
        take(*slot)

    for step in range(1, 16):
        rhs_to(step).wait_recv()
    total = rhs_all[0]
    for step in range(1, 16):
        total = total + rhs_all[step]
    rhs[...] = (total * rhs_scale).reshape(COLS)

    late_sums((near % 2) == 0)
    @pl.when(near != 0)
    def _():
        pass_over(0)

    keep_near(0)
    last_sums(1, (near % 2) == 1)
    late_sums((near % 2) == 1)
    add_on(0)
    pass_over(1, 0)
    hand_on(0)
    keep_near(1, 0)
    add_on(1, 0)
    hand_on(1, 0)
    for m in range(2):
        total = summed(m, kept, 1, 1)

        @pl.when(settled)
        def _():
            own[m, 1, span(1)] = total

        @pl.when(jnp.logical_not(settled))
        def _():
            leaving[1, m, 1, span(1)] = total.astype(BF16)
            z_on(m, 1, 1).start()

    def place(m, c, e, total):
        first, count = m * PART + (128 if e == 1 else 0), PART if e is None else 128
        for b in range(4):
            to = pl.ds(b // 2 * 512 + b % 2 * 256 + c * 128, 128)
            normal[pl.ds(first, count), to] = total[:, b * 128 : b * 128 + 128] * scale

    for c, e in ((0, None), (1, 0), (1, 1)):
        for m in range(2):

            @pl.when(settled)
            def _():
                total = own[m, c, span(e)]
                if e != 1:
                    z_home(m, c, e).wait_recv()
                    total = total + landed[0, m, c, span(e)].astype(F32)
                place(m, c, e, total)

            @pl.when(jnp.logical_not(settled))
            def _():
                z_on(m, c, e).wait_recv()
                total = landed[0, m, c, span(e)].astype(F32)
                if m == 1 and e != 1:
                    z_fwd(c, e).wait_recv()
                    total = total + landed[1, 1, c, span(e)].astype(F32)
                place(m, c, e, total)

    @pl.when(o < 15)
    def _():
        for copy in halo_copies():
            copy.wait_send()

    for m in range(2):
        for e in range(2):
            rows_over(m, e).wait_send()
        cols_over(m).wait_send()
        cols_across(m).wait_send()
        cols_on(m).wait_send()
        z_on(m, 0).wait_send()
        z_on(m, 1, 0).wait_send()
        swap_own(m).wait_send()
        for role in range(1, 4):
            swap(role, m).wait_send()

        @pl.when(settled)
        def _():
            z_fwd(m, first_of(m)).wait_send()

        @pl.when(jnp.logical_not(settled))
        def _():
            z_on(m, 1, 1).wait_send()
            z_home(m, 0).wait_send()
            z_home(m, 1, 0).wait_send()

        for q in range(4):
            x_far(m, q, first_of(q)).wait_send()
            x_raw(m, q, first_of(q)).wait_send()
            x_sum(m, q, first_of(q)).wait_send()
        x_far(m, kept, 1, 1).wait_send()
        x_raw(m, kept, 1, 1).wait_send()
        x_sum(m, kept, 1, 1).wait_send()
    for copy in first_pieces() + passed_on() + second_pieces():
        copy.wait_send()
    for step in range(1, 16):
        rhs_to(step).wait_send()


def per_device(design, observed, row_weight, taps):
    total_rows = ROWS * lax.axis_size("obs")
    dma = pltpu.SemaphoreType.DMA
    vmem = pl.BlockSpec(memory_space=pltpu.VMEM)
    normal, rhs, filtered_obs = pl.pallas_call(
        functools.partial(kernel, 1.0 / total_rows, 1.0 / math.sqrt(total_rows)),
        out_shape=(
            jax.ShapeDtypeStruct((512, COLS), F32),
            jax.ShapeDtypeStruct((COLS,), F32),
            jax.ShapeDtypeStruct((ROWS,), F32),
        ),
        in_specs=[pl.BlockSpec(memory_space=pl.ANY), vmem, vmem, pl.BlockSpec(memory_space=pltpu.SMEM)],
        out_specs=(vmem, vmem, vmem),
        scratch_shapes=[
            pltpu.VMEM((ROWS, COLS), BF16),
            pltpu.VMEM((ROWS + 8, COLS), F32),
            pltpu.VMEM((16, COLS), BF16),
            pltpu.VMEM((8, 128), F32),
            pltpu.VMEM((8, 128), F32),
            pltpu.VMEM((ROWS, 128), F32),
            pltpu.VMEM((2, 2, PART, ROWS), BF16),
            pltpu.VMEM((16, ROWS), BF16),
            pltpu.VMEM((4, 2, PART, DEPTH), BF16),
            pltpu.VMEM((2, 2, DEPTH, 512), BF16),
            pltpu.VMEM((3, 2, 4, PART, 512), BF16),
            pltpu.VMEM((2, 4, PART, 512), F32),
            pltpu.VMEM((2, 2, 4, PART, 512), BF16),
            pltpu.VMEM((2, 4, PART, 512), BF16),
            pltpu.VMEM((2, 128, 512), BF16),
            pltpu.VMEM((4, 2, 128, 512), BF16),
            pltpu.VMEM((2, 2, 2, PART, 512), BF16),
            pltpu.VMEM((2, 2, 2, PART, 512), BF16),
            pltpu.VMEM((2, PART, 512), BF16),
            pltpu.VMEM((16, 8, 128), F32),
            dma, dma((2,)), dma((2,)),
            dma((2, 2, 2, 2)), dma((2, 2, 2)), dma((2, 2)), dma((4, 2, 2, 2)),
            dma((2,)), dma((2,)), dma((2,)), dma((2, 2, 2)),
            dma((2, 6, 4)), dma((2, 6, 4)), dma((4, 2)), dma((4, 2)),
            dma((2, 2, 3)), dma((2, 2, 3)), dma((3,)), dma((3,)),
            dma((16,)), dma((16,)),
        ],
        compiler_params=pltpu.CompilerParams(collective_id=0, has_side_effects=True, vmem_limit_bytes=60 << 20),
        name="normal_equations",
    )(design, observed, row_weight, taps)
    return normal, rhs, filtered_obs


def solution(mesh):
    placed = (P("obs", "param"), P("obs"), P("obs"), P())
    return jax.shard_map(
        per_device,
        mesh=mesh,
        in_specs=placed,
        out_specs=(P("obs", "param"), P("param"), P("obs")),
        check_vma=False,
    )
```

```python
import functools
import math

import jax
import jax.numpy as jnp
from jax import lax
from jax.experimental import pallas as pl
from jax.experimental.pallas import tpu as pltpu
from jax.sharding import PartitionSpec as P

MESH = pl.DeviceIdType.MESH
BF16, F32 = jnp.bfloat16, jnp.float32
ROWS = 640
COLS = 1024
LAGS = 7
PART = 256
DEPTH = 2 * ROWS


def kernel(
    scale, rhs_scale,
    design_hbm, observed, weight, taps,
    normal, rhs, filtered_obs,
    design, ext, halo, obs_tail, obs_halo, wcol, mine, weighted, rows, cols, part, own, taken, far, giving, swapped,
    leaving, landed, passing, result, small_obs, small_rhs, rhs_all,
    design_s, out_s, small_s, halo_s, halo_r, rows_s, rows_f, rows_sib, rows_r, cols_s, cols_sib, cols_f, cols_r, x_s, x_r, swap_s, swap_r, z_s, z_r, z_fs, z_fr, rhs_s, rhs_r,
):
    p, o = lax.axis_index("param"), lax.axis_index("obs")
    y, h = p // 2, p % 2
    x, l, k = o // 4, (o // 2) % 2, o % 2
    near = (y - x + 4) % 4
    settled = l == h
    kept, given = jnp.where(settled, 1, 3), jnp.where(settled, 3, 1)

    def param_of(y_, h_):
        return ((y_ + 4) % 4) * 2 + h_

    def obs_of(x_, l_, k_):
        return ((x_ + 4) % 4) * 4 + l_ * 2 + k_

    sibling = (p, obs_of(x, l, 1 - k))
    across = (param_of(y, 1 - h), o)
    beside = (p, obs_of(x, 1 - l, k))
    corner = (param_of(y, 1 - h), obs_of(x, 1 - l, k))
    following = (p, (o + 1) % 16)

    def remote(src, dst, send, recv, device):
        return pltpu.make_async_remote_copy(
            src_ref=src, dst_ref=dst, send_sem=send, recv_sem=recv, device_id=device, device_id_type=MESH
        )

    def halo_copies():
        return (
            remote(design.at[pl.ds(ROWS - 16, 16), :], halo, halo_s.at[0], halo_r.at[0], following),
            remote(obs_tail, obs_halo, halo_s.at[1], halo_r.at[1], following),
        )

    def lanes(rel):
        return pl.ds(ROWS * rel, ROWS)

    def span(e):
        return pl.ds(0, PART) if e is None else pl.ds(pl.multiple_of(e * 128, 128), 128)

    def wide(c):
        return pl.ds(c * 512, 512)

    def rows_out(m, rel, e, up, begin=0, end=ROWS):
        target = (param_of(y + 2 * up - 1, h), obs_of(x, l, (k + rel) % 2))
        dy = 1 + 2 * up
        to = pl.ds(pl.multiple_of(ROWS * rel + begin, 128), end - begin)
        return remote(
            mine.at[rel, m, span(e), pl.ds(begin, end - begin)], rows.at[dy, m, span(e), to],
            rows_s.at[up, m, rel, e], rows_r.at[dy, m, rel, e], target,
        )

    def rows_on(m, rel, e):
        target = (param_of(y + 1 - 2 * m, h), o)
        return remote(
            rows.at[3 - 2 * m, m, span(e), lanes(rel)], rows.at[2, m, span(e), lanes(rel)],
            rows_f.at[m, rel, e], rows_r.at[2, m, rel, e], target,
        )

    def rows_at(dy, m, rel, e):
        piece = rows.at[dy, m, span(e), lanes(rel)]
        return remote(piece, piece, rows_f.at[0, 0, 0], rows_r.at[dy, m, rel, e], following)

    def rows_over(m, e):
        return remote(mine.at[1, m, span(e)], rows.at[0, m, span(e), lanes(1)], rows_sib.at[m, e], rows_r.at[0, m, 1, e], sibling)

    def cols_over(n, begin=0, end=ROWS):
        half, other = pl.ds(begin, end - begin), pl.ds(ROWS + begin, end - begin)
        return remote(cols.at[0, n, half, :], cols.at[0, n, other, :], cols_sib.at[n], cols_r.at[0, n, 1], sibling)

    def cols_across(n, begin=0, end=ROWS):
        half = pl.ds(begin, end - begin)
        return remote(cols.at[0, n, half, :], cols.at[1, n, half, :], cols_s.at[n], cols_r.at[1, n, 0], across)

    def cols_on(n):
        half = pl.ds(0, ROWS)
        return remote(cols.at[1, n, half, :], cols.at[1, n, pl.ds(ROWS, ROWS), :], cols_f.at[n], cols_r.at[1, n, 1], sibling)

    def beyond(d):
        return (p, obs_of(x + 1 - 2 * d, l, k))

    def x_far(d, q, e=None, late=0):
        at = span(e)
        return remote(part.at[1, d, q, at], far.at[d, q, at], x_s.at[d, 3 * late, q], x_r.at[d, 3 * late, q], beyond(d))

    def x_raw(d, q, e=None, late=0):
        at, kind = span(e), 1 + 3 * late
        dst = taken.at[d, 1 - d, q, at]
        return remote(part.at[2 * d, 1 - d, q, at], dst, x_s.at[d, kind, q], x_r.at[d, kind, q], beyond(d))

    def x_sum(d, q, e=None, late=0):
        at, kind = span(e), 2 + 3 * late
        return remote(part.at[2 * d, d, q, at], taken.at[d, d, q, at], x_s.at[d, kind, q], x_r.at[d, kind, q], beyond(d))

    def swap(role, m):
        place = part.at[role - 1, m, given, span(1)]
        return remote(place, swapped.at[role, m], swap_s.at[role, m], swap_r.at[role, m], beside)

    def swap_own(m):
        return remote(giving.at[m], swapped.at[0, m], swap_s.at[0, m], swap_r.at[0, m], beside)

    def z_home(m, c, e=None):
        sem = step_of(c, e)
        return remote(leaving.at[0, m, c, span(e)], landed.at[0, m, c, span(e)], z_s.at[0, m, sem], z_r.at[0, m, sem], beside)

    def step_of(c, e):
        return c if e is None else c + e

    def z_add(c, e=None):
        sem, at = step_of(c, e), span(e)
        return remote(leaving.at[1, 0, c, at], landed.at[1, 0, c, at], z_s.at[1, 0, sem], z_r.at[1, 0, sem], beside)

    def z_on(m, c, e=None):
        sem, at = step_of(c, e), span(e)
        return remote(leaving.at[1, m, c, at], landed.at[0, m, c, at], z_s.at[1, m, sem], z_r.at[0, m, sem], corner)

    def z_via(c, e=None):
        sem, at = step_of(c, e), span(e)
        return remote(leaving.at[1, 1, c, at], passing.at[c, at], z_s.at[1, 1, sem], z_r.at[1, 1, sem], corner)

    def z_fwd(c, e=None):
        sem, at = step_of(c, e), span(e)
        return remote(passing.at[c, at], landed.at[1, 1, c, at], z_fs.at[sem], z_fr.at[sem], beside)

    def obs_out():
        return pltpu.make_async_copy(small_obs, filtered_obs, small_s.at[0])

    def rhs_out():
        return pltpu.make_async_copy(small_rhs, rhs, small_s.at[1])

    def rhs_to(step):
        peer = (p, (o + step) % 16)
        return remote(rhs_all.at[o], rhs_all.at[o], rhs_s.at[step], rhs_r.at[step], peer)

    incoming = pltpu.make_async_copy(design_hbm, design, design_s)
    incoming.start()

    barrier = pltpu.get_barrier_semaphore()
    greeted = [(param_of(y + step, h), obs_of(x, l, core)) for step in (1, -1) for core in (k, 1 - k)] + [across, corner]
    greeted += [(p, (o + step) % 16) for step in range(1, 16)]
    for device in greeted:
        pl.semaphore_signal(barrier, inc=1, device_id=device, device_id_type=MESH)

    signal_row = jnp.broadcast_to(observed[...].astype(F32).reshape(1, ROWS), (8, ROWS))
    weight_row = jnp.broadcast_to(weight[...].reshape(1, ROWS), (8, ROWS))
    obs_tail[...] = signal_row[:, ROWS - 128 :]
    for r in range(ROWS // 128):
        block = jnp.broadcast_to(weight_row[0:1, r * 128 : (r + 1) * 128], (128, 128))
        wcol[pl.ds(r * 128, 128), :] = block.T

    def order(i):
        return i // 4, i % 2, 1 - (i // 2) % 2

    def filter_rows(i, r):
        e, m, rel = order(i)
        core = (k + rel) % 2
        at = pl.ds(pl.multiple_of(core * 512 + m * PART + e * 128, 128), 128)
        quarter = pl.ds(pl.multiple_of((core * 2 + m) * 128, 128), 128)
        first = r * 128
        total = ext[pl.ds(8 + first, 128), at]
        for lag in range(1, LAGS + 1):
            total = total + taps[lag - 1] * ext[pl.ds(8 + first - lag, 128), at]
        rounded = total.astype(BF16).astype(F32)
        cols[0, e, pl.ds(first, 128), quarter] = (wcol[pl.ds(first, 128), :] * rounded).astype(BF16)
        turned = rounded.T.astype(BF16)
        mine[rel, m, span(e), pl.ds(first, 128)] = turned

        @pl.when(rel == 0)
        def _():
            rows[0, m, span(e), pl.ds(first, 128)] = turned

    def filter_later_rows(i, _):
        e, m, rel = order(i)
        at = pl.ds(pl.multiple_of((k + rel) % 2 * 512 + m * PART + e * 128, 128), 128)
        ext[pl.ds(8, ROWS), at] = design[:, at].astype(F32)
        for r in range(1, ROWS // 128):
            filter_rows(i, r)
        return 0

    incoming.wait()
    lax.fori_loop(0, 2, filter_later_rows, 0)
    pl.semaphore_wait(barrier, len(greeted))

    @pl.when(o < 15)
    def _():
        for copy in halo_copies():
            copy.start()

    def start_early(i, _):
        e, m, rel = order(i)
        rows_out(m, rel, 0, 1 - m, 128).start()
        return 0

    def filter_and_start(i, _):
        filter_later_rows(i, _)
        return start_early(i, _)

    lax.fori_loop(0, 2, start_early, 0)
    lax.fori_loop(2, 4, filter_and_start, 0)
    cols_across(0, 128).start()
    cols_over(0, 128).start()
    lax.fori_loop(4, 8, filter_later_rows, 0)

    @pl.when(o > 0)
    def _():
        for copy in halo_copies():
            copy.wait_recv()
        ext[pl.ds(0, 8), :] = halo[...].astype(F32)[8:]

    @pl.when(o == 0)
    def _():
        ext[pl.ds(0, 8), :] = jnp.zeros((8, COLS), F32)
        obs_halo[...] = jnp.zeros((8, 128), F32)

    def first_pieces():
        return [rows_out(m, rel, e, 1 - m) for e in range(2) for m in range(2) for rel in (1, 0)]

    def second_pieces():
        return [rows_out(m, rel, e, m) for e in range(2) for m in range(2) for rel in (1, 0)]

    def passed_on(halves=(0, 1)):
        return [rows_on(m, rel, e) for e in halves for m in range(2) for rel in (1, 0)]

    def arrived(dy, m):
        for rel in (1, 0):
            for e in range(2):
                rows_at(dy, m, rel, e).wait_recv()

    def filter_block(i, _):
        e, m, rel = order(i)
        filter_rows(i, 0)

        @pl.when(e == 0)
        def _():
            rows_out(m, rel, e, 1 - m, 0, 128).start()

        @pl.when(e == 1)
        def _():
            rows_out(m, rel, e, 1 - m).start()

        @pl.when(rel == 1)
        def _():
            rows_over(m, e).start()

        @pl.when(i == 3)
        def _():
            cols_across(0, 0, 128).start()
            cols_over(0, 0, 128).start()

        return 0

    lax.fori_loop(0, 8, filter_block, 0)
    cols_across(1).start()
    cols_over(1).start()
    first_far = near == 2

    @pl.when(first_far)
    def _():
        for copy in second_pieces():
            copy.start()

    def multiply(dy, m, q, e=None):
        role = (near + dy) % 4

        def chunk(c, _):
            at = pl.ds(pl.multiple_of(c * 256, 256), 256)
            value = jnp.dot(rows[dy, m, span(e)], cols[q // 2, q % 2, :, at], preferred_element_type=F32)

            @pl.when(role == 0)
            def _():
                own[m, q, span(e), at] = value

            @pl.when(role != 0)
            def _():
                part[role - 1, m, q, span(e), at] = value.astype(BF16)

            return 0

        lax.fori_loop(0, 2, chunk, 0)

        if q % 2 == 1 and e == 1:
            return
        e = 0 if q % 2 == 1 else e

        @pl.when(role == 2)
        def _():
            x_far(m, q, e).start()

        @pl.when(as_it_is(role, m))
        def _():
            x_raw(role // 2, q, e).start()

    def as_it_is(role, m):
        return jnp.logical_or(jnp.logical_and(role == 1, m == 1), jnp.logical_and(role == 3, m == 0))

    def give(dy, m):
        role = (near + dy) % 4

        @pl.when(role == 0)
        def _():
            giving[m] = own[m, given, span(1)].astype(BF16)
            swap_own(m).start()

        @pl.when(role != 0)
        def _():
            swap(role, m).start()

    def take(dy, m):
        role = (near + dy) % 4

        @pl.when(role == 0)
        def _():
            swap_own(m).wait_recv()
            own[m, kept, span(1)] = own[m, kept, span(1)] + swapped[0, m].astype(F32)

        @pl.when(role != 0)
        def _():
            swap(role, m).wait_recv()
            both = part[role - 1, m, kept, span(1)].astype(F32) + swapped[role, m].astype(F32)
            part[role - 1, m, kept, span(1)] = both.astype(BF16)

        @pl.when(role == 2)
        def _():
            x_far(m, kept, 1, 1).start()

        @pl.when(as_it_is(role, m))
        def _():
            x_raw(role // 2, kept, 1, 1).start()

    def add_far(d, q, valid=True, late=0):
        e = late if late else first_of(q)

        @pl.when(valid)
        def _():
            x_far(d, q, e, late).wait_recv()
            both = part[2 * d, d, q, span(e)].astype(F32) + far[d, q, span(e)].astype(F32)
            part[2 * d, d, q, span(e)] = both.astype(BF16)
            x_sum(d, q, e, late).start()

    def first_of(q):
        return 0 if q % 2 == 1 else None

    def by_near(*values):
        chosen = values[3]
        for place in (2, 1, 0):
            chosen = jnp.where(near == place, values[place], chosen)
        return chosen

    for m in range(2):
        for e in range(2):
            rows_over(m, e).wait_recv()
        cols_over(m).wait_recv()
    for q in range(2):
        for m in (1, 0):
            multiply(0, m, q)

    for e in range(2):
        for m in range(2):
            for rel in (1, 0):
                rows_at(3 - 2 * m, m, rel, e).wait_recv()
        for copy in passed_on((e,)):
            copy.start()
        if e == 1:

            @pl.when(jnp.logical_not(first_far))
            def _():
                for copy in second_pieces():
                    copy.start()

        for q in range(2):
            multiply(3, 0, q, e)
            multiply(1, 1, q, e)
        add_far(by_near(0, 0, 0, 1), e, (near % 2) == 1)
    cols_across(0).wait_recv()
    cols_on(0).start()
    cols_on(0).wait_recv()
    multiply(by_near(3, 0, 0, 0), by_near(0, 1, 1, 1), 2)
    multiply(by_near(1, 0, 0, 0), by_near(1, 0, 0, 0), 2)
    multiply(by_near(0, 3, 3, 3), by_near(1, 0, 0, 0), 2)
    multiply(by_near(0, 1, 1, 1), by_near(0, 1, 1, 1), 2)
    for q in range(2):
        for d in range(2):
            add_far(d, q, near == 2)

    extended = jnp.concatenate([obs_halo[...], signal_row], axis=1)
    total = signal_row
    for lag in range(1, LAGS + 1):
        total = total + taps[lag - 1] * pltpu.roll(extended, lag, 1)[:, 128:]
    small_obs[...] = total[0:1, :].reshape(ROWS)
    obs_out().start()
    weighted[...] = jnp.concatenate([weight_row * total, weight_row * total], axis=0).astype(BF16)
    line = lax.broadcasted_iota(jnp.int32, (8, 128), 0)
    sums = jnp.zeros((8, 128), F32)
    for m in range(2):
        for rel in range(2):
            core = (k + rel) % 2
            dots = lax.dot_general(weighted[...], mine[rel, m], (((1,), (1,)), ((), ())), preferred_element_type=F32)
            for c in range(2):
                sums = jnp.where(line == core * 4 + m * 2 + c, dots[0:8, c * 128 : (c + 1) * 128], sums)
    rhs_all[o] = sums
    for step in range(1, 16):
        rhs_to(step).start()

    third = (by_near(2, 1, 2, 3), by_near(0, 0, 0, 1))
    fourth = (2, by_near(1, 0, 1, 1))
    fifth = (by_near(1, 2, 1, 2), by_near(0, 1, 0, 0))
    sixth = (by_near(3, 3, 3, 1), by_near(1, 1, 1, 0))
    arrived(*third)
    multiply(*third, 2)
    arrived(*fourth)
    multiply(*fourth, 2)
    for q in (0, 1):
        multiply(*third, q)
        multiply(*fourth, q)
    cols_across(1).wait_recv()
    cols_on(1).start()
    cols_on(1).wait_recv()

    def last_sums(q, valid=True):
        add_far(by_near(0, 1, 0, 0), q, valid)
        add_far(1, q, jnp.logical_and(valid, (near % 2) == 0))

    slots = (
        (by_near(2, 1, 0, 3), by_near(0, 0, 1, 1)),
        (by_near(2, 1, 0, 3), by_near(1, 1, 0, 0)),
        (by_near(3, 0, 3, 0), by_near(0, 0, 0, 1)),
        (by_near(1, 0, 1, 0), by_near(1, 1, 1, 0)),
        (by_near(0, 2, 2, 2), by_near(0, 0, 0, 1)),
        (by_near(0, 3, 2, 1), by_near(1, 0, 1, 1)),
    )
    def summed(m, q, e=None, late=0):
        x_sum(m, q, e, late).wait_recv()
        x_raw(1 - m, q, e, late).wait_recv()
        return own[m, q, span(e)] + taken[0, m, q, span(e)].astype(F32) + taken[1, m, q, span(e)].astype(F32)

    def keep_near(c, e=None):
        for m in range(2):
            total = summed(m, c, e)

            @pl.when(settled)
            def _():
                own[m, c, span(e)] = total

            @pl.when(jnp.logical_not(settled))
            def _():
                leaving[0, m, c, span(e)] = total.astype(BF16)
                z_home(m, c, e).start()

    def pass_over(c, e=None):
        for m in (1, 0):
            total = summed(m, 2 + c, e)

            @pl.when(settled)
            def _():
                leaving[1, m, c, span(e)] = total.astype(BF16)
                (z_add(c, e) if m == 0 else z_via(c, e)).start()

            @pl.when(jnp.logical_not(settled))
            def _():
                if m == 0:
                    own[m, 2 + c, span(e)] = total
                else:
                    leaving[1, m, c, span(e)] = total.astype(BF16)
                    z_on(m, c, e).start()

    def hand_on(c, e=None):
        @pl.when(settled)
        def _():
            z_via(c, e).wait_recv()
            z_fwd(c, e).start()

    def add_on(c, e=None):
        @pl.when(jnp.logical_not(settled))
        def _():
            z_add(c, e).wait_recv()
            leaving[1, 0, c, span(e)] = (own[0, 2 + c, span(e)] + landed[1, 0, c, span(e)].astype(F32)).astype(BF16)
            z_on(0, c, e).start()

    def late_sums(valid):
        for d in range(2):
            add_far(d, kept, valid, 1)

    for slot in slots[0:2]:
        multiply(*slot, 3)
        give(*slot)
    add_far(by_near(0, 0, 0, 1), 2, near != 0)
    add_far(1, 2, near == 2)
    for slot in slots[2:6]:
        multiply(*slot, 3)
        give(*slot)
    for piece in (fifth, sixth):
        arrived(*piece)
    for piece in (fifth, sixth):
        multiply(*piece, 2)
    last_sums(2, near != 2)
    for slot in slots[0:2]:
        take(*slot)
    for piece in (fifth, sixth):
        multiply(*piece, 0)
    last_sums(0, near != 2)
    add_far(by_near(0, 0, 0, 1), 3, (near % 2) == 1)
    for piece in (fifth, sixth):
        multiply(*piece, 3)
        multiply(*piece, 1)
        give(*piece)
    for slot in slots[2:4]:
        take(*slot)
    last_sums(3)
    last_sums(1, near == 0)

    @pl.when(near == 0)
    def _():
        pass_over(0)

    for slot in slots[4:6] + (fifth, sixth):
        take(*slot)

    for step in range(1, 16):
        rhs_to(step).wait_recv()
    total = rhs_all[0]
    for step in range(1, 16):
        total = total + rhs_all[step]
    small_rhs[...] = (total * rhs_scale).reshape(COLS)
    rhs_out().start()

    late_sums((near % 2) == 0)
    @pl.when(near != 0)
    def _():
        pass_over(0)

    keep_near(0)
    last_sums(1, (near % 2) == 1)
    late_sums((near % 2) == 1)
    add_on(0)
    pass_over(1, 0)
    hand_on(0)
    keep_near(1, 0)
    add_on(1, 0)
    hand_on(1, 0)
    for m in range(2):
        total = summed(m, kept, 1, 1)

        @pl.when(settled)
        def _():
            own[m, 1, span(1)] = total

        @pl.when(jnp.logical_not(settled))
        def _():
            leaving[1, m, 1, span(1)] = total.astype(BF16)
            z_on(m, 1, 1).start()

    obs_out().wait()
    rhs_out().wait()
    @pl.when(o < 15)
    def _():
        for copy in halo_copies():
            copy.wait_send()

    for m in range(2):
        for e in range(2):
            rows_over(m, e).wait_send()
        cols_over(m).wait_send()
        cols_across(m).wait_send()
        cols_on(m).wait_send()
        swap_own(m).wait_send()
        for role in range(1, 4):
            swap(role, m).wait_send()
        for q in range(4):
            x_far(m, q, first_of(q)).wait_send()
            x_raw(m, q, first_of(q)).wait_send()
            x_sum(m, q, first_of(q)).wait_send()
        x_far(m, kept, 1, 1).wait_send()
        x_raw(m, kept, 1, 1).wait_send()
        x_sum(m, kept, 1, 1).wait_send()
    for copy in first_pieces() + passed_on() + second_pieces():
        copy.wait_send()
    for step in range(1, 16):
        rhs_to(step).wait_send()

    def place(m, c, e, total):
        first, count = m * PART + (128 if e == 1 else 0), PART if e is None else 128
        for b in range(4):
            to = pl.ds(b // 2 * 512 + b % 2 * 256 + c * 128, 128)
            result[pl.ds(first, count), to] = total[:, b * 128 : b * 128 + 128] * scale
        if c == 1:
            leave(m, e).start()

    def leave(m, e):
        half = pl.ds(m * PART + 128 * e, 128)
        return pltpu.make_async_copy(result.at[half], normal.at[half], out_s.at[m, e])

    for c, e in ((0, None), (1, 0), (1, 1)):
        for m in range(2):

            @pl.when(settled)
            def _():
                total = own[m, c, span(e)]
                if e != 1:
                    z_home(m, c, e).wait_recv()
                    total = total + landed[0, m, c, span(e)].astype(F32)
                place(m, c, e, total)

            @pl.when(jnp.logical_not(settled))
            def _():
                z_on(m, c, e).wait_recv()
                total = landed[0, m, c, span(e)].astype(F32)
                if m == 1 and e != 1:
                    z_fwd(c, e).wait_recv()
                    total = total + landed[1, 1, c, span(e)].astype(F32)
                place(m, c, e, total)

    for m in range(2):
        for e in range(2):
            leave(m, e).wait()
    for m in range(2):
        z_on(m, 0).wait_send()
        z_on(m, 1, 0).wait_send()

        @pl.when(settled)
        def _():
            z_fwd(m, first_of(m)).wait_send()

        @pl.when(jnp.logical_not(settled))
        def _():
            z_on(m, 1, 1).wait_send()
            z_home(m, 0).wait_send()
            z_home(m, 1, 0).wait_send()


def per_device(design, observed, row_weight, taps):
    total_rows = ROWS * lax.axis_size("obs")
    dma = pltpu.SemaphoreType.DMA
    vmem = pl.BlockSpec(memory_space=pltpu.VMEM)
    normal, rhs, filtered_obs = pl.pallas_call(
        functools.partial(kernel, 1.0 / total_rows, 1.0 / math.sqrt(total_rows)),
        out_shape=(
            jax.ShapeDtypeStruct((512, COLS), F32),
            jax.ShapeDtypeStruct((COLS,), F32),
            jax.ShapeDtypeStruct((ROWS,), F32),
        ),
        in_specs=[pl.BlockSpec(memory_space=pl.ANY), vmem, vmem, pl.BlockSpec(memory_space=pltpu.SMEM)],
        out_specs=(pl.BlockSpec(memory_space=pl.ANY),) * 3,
        scratch_shapes=[
            pltpu.VMEM((ROWS, COLS), BF16),
            pltpu.VMEM((ROWS + 8, COLS), F32),
            pltpu.VMEM((16, COLS), BF16),
            pltpu.VMEM((8, 128), F32),
            pltpu.VMEM((8, 128), F32),
            pltpu.VMEM((ROWS, 128), F32),
            pltpu.VMEM((2, 2, PART, ROWS), BF16),
            pltpu.VMEM((16, ROWS), BF16),
            pltpu.VMEM((4, 2, PART, DEPTH), BF16),
            pltpu.VMEM((2, 2, DEPTH, 512), BF16),
            pltpu.VMEM((3, 2, 4, PART, 512), BF16),
            pltpu.VMEM((2, 4, PART, 512), F32),
            pltpu.VMEM((2, 2, 4, PART, 512), BF16),
            pltpu.VMEM((2, 4, PART, 512), BF16),
            pltpu.VMEM((2, 128, 512), BF16),
            pltpu.VMEM((4, 2, 128, 512), BF16),
            pltpu.VMEM((2, 2, 2, PART, 512), BF16),
            pltpu.VMEM((2, 2, 2, PART, 512), BF16),
            pltpu.VMEM((2, PART, 512), BF16),
            pltpu.VMEM((512, COLS), F32),
            pltpu.VMEM((ROWS,), F32),
            pltpu.VMEM((COLS,), F32),
            pltpu.VMEM((16, 8, 128), F32),
            dma, dma((2, 2)), dma((2,)), dma((2,)), dma((2,)),
            dma((2, 2, 2, 2)), dma((2, 2, 2)), dma((2, 2)), dma((4, 2, 2, 2)),
            dma((2,)), dma((2,)), dma((2,)), dma((2, 2, 2)),
            dma((2, 6, 4)), dma((2, 6, 4)), dma((4, 2)), dma((4, 2)),
            dma((2, 2, 3)), dma((2, 2, 3)), dma((3,)), dma((3,)),
            dma((16,)), dma((16,)),
        ],
        compiler_params=pltpu.CompilerParams(collective_id=0, has_side_effects=True, vmem_limit_bytes=60 << 20),
        name="normal_equations",
    )(design, observed, row_weight, taps)
    return normal, rhs, filtered_obs


def solution(mesh):
    placed = (P("obs", "param"), P("obs"), P("obs"), P())
    return jax.shard_map(
        per_device,
        mesh=mesh,
        in_specs=placed,
        out_specs=(P("obs", "param"), P("param"), P("obs")),
        check_vma=False,
    )
```

```python
import functools
import math

import jax
import jax.numpy as jnp
from jax import lax
from jax.experimental import pallas as pl
from jax.experimental.pallas import tpu as pltpu
from jax.sharding import PartitionSpec as P

MESH = pl.DeviceIdType.MESH
BF16, F32 = jnp.bfloat16, jnp.float32
ROWS = 640
COLS = 1024
LAGS = 7
PART = 256
DEPTH = 2 * ROWS


def kernel(
    scale, rhs_scale,
    design_hbm, observed, weight, taps,
    normal, rhs, filtered_obs,
    design, ext, halo, obs_tail, obs_halo, wcol, mine, weighted, rows, cols, part, own, taken, far, giving, swapped,
    leaving, landed, passing, result, small_obs, small_rhs, rhs_all,
    design_s, out_s, small_s, halo_s, halo_r, rows_s, rows_f, rows_sib, rows_r, cols_s, cols_sib, cols_f, cols_r, x_s, x_r, swap_s, swap_r, z_s, z_r, z_fs, z_fr, rhs_s, rhs_r,
):
    p, o = lax.axis_index("param"), lax.axis_index("obs")
    y, h = p // 2, p % 2
    x, l, k = o // 4, (o // 2) % 2, o % 2
    near = (y - x + 4) % 4
    settled = l == h
    kept, given = jnp.where(settled, 1, 3), jnp.where(settled, 3, 1)

    def param_of(y_, h_):
        return ((y_ + 4) % 4) * 2 + h_

    def obs_of(x_, l_, k_):
        return ((x_ + 4) % 4) * 4 + l_ * 2 + k_

    sibling = (p, obs_of(x, l, 1 - k))
    across = (param_of(y, 1 - h), o)
    beside = (p, obs_of(x, 1 - l, k))
    corner = (param_of(y, 1 - h), obs_of(x, 1 - l, k))
    following = (p, (o + 1) % 16)

    def remote(src, dst, send, recv, device):
        return pltpu.make_async_remote_copy(
            src_ref=src, dst_ref=dst, send_sem=send, recv_sem=recv, device_id=device, device_id_type=MESH
        )

    def halo_copies():
        return (
            remote(design.at[pl.ds(ROWS - 16, 16), :], halo, halo_s.at[0], halo_r.at[0], following),
            remote(obs_tail, obs_halo, halo_s.at[1], halo_r.at[1], following),
        )

    def lanes(rel):
        return pl.ds(ROWS * rel, ROWS)

    def span(e):
        return pl.ds(0, PART) if e is None else pl.ds(pl.multiple_of(e * 128, 128), 128)

    def wide(c):
        return pl.ds(c * 512, 512)

    def rows_out(m, rel, e, up, begin=0, end=ROWS):
        target = (param_of(y + 2 * up - 1, h), obs_of(x, l, (k + rel) % 2))
        dy = 1 + 2 * up
        to = pl.ds(pl.multiple_of(ROWS * rel + begin, 128), end - begin)
        return remote(
            mine.at[rel, m, span(e), pl.ds(begin, end - begin)], rows.at[dy, m, span(e), to],
            rows_s.at[up, m, rel, e], rows_r.at[dy, m, rel, e], target,
        )

    def rows_on(m, rel, e):
        target = (param_of(y + 1 - 2 * m, h), o)
        return remote(
            rows.at[3 - 2 * m, m, span(e), lanes(rel)], rows.at[2, m, span(e), lanes(rel)],
            rows_f.at[m, rel, e], rows_r.at[2, m, rel, e], target,
        )

    def rows_at(dy, m, rel, e):
        piece = rows.at[dy, m, span(e), lanes(rel)]
        return remote(piece, piece, rows_f.at[0, 0, 0], rows_r.at[dy, m, rel, e], following)

    def rows_over(m, e):
        return remote(mine.at[1, m, span(e)], rows.at[0, m, span(e), lanes(1)], rows_sib.at[m, e], rows_r.at[0, m, 1, e], sibling)

    def cols_over(n, begin=0, end=ROWS):
        half, other = pl.ds(begin, end - begin), pl.ds(ROWS + begin, end - begin)
        return remote(cols.at[0, n, half, :], cols.at[0, n, other, :], cols_sib.at[n], cols_r.at[0, n, 1], sibling)

    def cols_across(n, begin=0, end=ROWS):
        half = pl.ds(begin, end - begin)
        return remote(cols.at[0, n, half, :], cols.at[1, n, half, :], cols_s.at[n], cols_r.at[1, n, 0], across)

    def cols_on(n):
        half = pl.ds(0, ROWS)
        return remote(cols.at[1, n, half, :], cols.at[1, n, pl.ds(ROWS, ROWS), :], cols_f.at[n], cols_r.at[1, n, 1], sibling)

    def beyond(d):
        return (p, obs_of(x + 1 - 2 * d, l, k))

    def x_far(d, q, e=None, late=0):
        at = span(e)
        return remote(part.at[1, d, q, at], far.at[d, q, at], x_s.at[d, 3 * late, q], x_r.at[d, 3 * late, q], beyond(d))

    def x_raw(d, q, e=None, late=0):
        at, kind = span(e), 1 + 3 * late
        dst = taken.at[d, 1 - d, q, at]
        return remote(part.at[2 * d, 1 - d, q, at], dst, x_s.at[d, kind, q], x_r.at[d, kind, q], beyond(d))

    def x_sum(d, q, e=None, late=0):
        at, kind = span(e), 2 + 3 * late
        return remote(part.at[2 * d, d, q, at], taken.at[d, d, q, at], x_s.at[d, kind, q], x_r.at[d, kind, q], beyond(d))

    def swap(role, m):
        place = part.at[role - 1, m, given, span(1)]
        return remote(place, swapped.at[role, m], swap_s.at[role, m], swap_r.at[role, m], beside)

    def swap_own(m):
        return remote(giving.at[m], swapped.at[0, m], swap_s.at[0, m], swap_r.at[0, m], beside)

    def z_home(m, c, e=None):
        sem = step_of(c, e)
        return remote(leaving.at[0, m, c, span(e)], landed.at[0, m, c, span(e)], z_s.at[0, m, sem], z_r.at[0, m, sem], beside)

    def step_of(c, e):
        return c if e is None else c + e

    def z_add(c, e=None):
        sem, at = step_of(c, e), span(e)
        return remote(leaving.at[1, 0, c, at], landed.at[1, 0, c, at], z_s.at[1, 0, sem], z_r.at[1, 0, sem], beside)

    def z_on(m, c, e=None):
        sem, at = step_of(c, e), span(e)
        return remote(leaving.at[1, m, c, at], landed.at[0, m, c, at], z_s.at[1, m, sem], z_r.at[0, m, sem], corner)

    def z_via(c, e=None):
        sem, at = step_of(c, e), span(e)
        return remote(leaving.at[1, 1, c, at], passing.at[c, at], z_s.at[1, 1, sem], z_r.at[1, 1, sem], corner)

    def z_fwd(c, e=None):
        sem, at = step_of(c, e), span(e)
        return remote(passing.at[c, at], landed.at[1, 1, c, at], z_fs.at[sem], z_fr.at[sem], beside)

    def obs_out():
        return pltpu.make_async_copy(small_obs, filtered_obs, small_s.at[0])

    def rhs_out():
        return pltpu.make_async_copy(small_rhs, rhs, small_s.at[1])

    def rhs_to(step):
        peer = (p, (o + step) % 16)
        return remote(rhs_all.at[o], rhs_all.at[o], rhs_s.at[step], rhs_r.at[step], peer)

    incoming = pltpu.make_async_copy(design_hbm, design, design_s)
    incoming.start()

    barrier = pltpu.get_barrier_semaphore()
    greeted = [(param_of(y + step, h), obs_of(x, l, core)) for step in (1, -1) for core in (k, 1 - k)] + [across, corner]
    greeted += [(p, (o + step) % 16) for step in range(1, 16)]
    for device in greeted:
        pl.semaphore_signal(barrier, inc=1, device_id=device, device_id_type=MESH)

    signal_row = jnp.broadcast_to(observed[...].astype(F32).reshape(1, ROWS), (8, ROWS))
    weight_row = jnp.broadcast_to(weight[...].reshape(1, ROWS), (8, ROWS))
    obs_tail[...] = signal_row[:, ROWS - 128 :]
    for r in range(ROWS // 128):
        block = jnp.broadcast_to(weight_row[0:1, r * 128 : (r + 1) * 128], (128, 128))
        wcol[pl.ds(r * 128, 128), :] = block.T

    def order(i):
        return i // 4, i % 2, 1 - (i // 2) % 2

    def filter_rows(i, r):
        e, m, rel = order(i)
        core = (k + rel) % 2
        at = pl.ds(pl.multiple_of(core * 512 + m * PART + e * 128, 128), 128)
        quarter = pl.ds(pl.multiple_of((core * 2 + m) * 128, 128), 128)
        first = r * 128
        total = ext[pl.ds(8 + first, 128), at]
        for lag in range(1, LAGS + 1):
            total = total + taps[lag - 1] * ext[pl.ds(8 + first - lag, 128), at]
        rounded = total.astype(BF16).astype(F32)
        cols[0, e, pl.ds(first, 128), quarter] = (wcol[pl.ds(first, 128), :] * rounded).astype(BF16)
        turned = rounded.T.astype(BF16)
        mine[rel, m, span(e), pl.ds(first, 128)] = turned

        @pl.when(rel == 0)
        def _():
            rows[0, m, span(e), pl.ds(first, 128)] = turned

    def filter_later_rows(i, _):
        e, m, rel = order(i)
        at = pl.ds(pl.multiple_of((k + rel) % 2 * 512 + m * PART + e * 128, 128), 128)
        ext[pl.ds(8, ROWS), at] = design[:, at].astype(F32)
        for r in range(1, ROWS // 128):
            filter_rows(i, r)
        return 0

    incoming.wait()
    lax.fori_loop(0, 2, filter_later_rows, 0)
    pl.semaphore_wait(barrier, len(greeted))

    @pl.when(o < 15)
    def _():
        for copy in halo_copies():
            copy.start()

    def start_early(i, _):
        e, m, rel = order(i)
        rows_out(m, rel, 0, 1 - m, 128).start()
        return 0

    def filter_and_start(i, _):
        filter_later_rows(i, _)
        return start_early(i, _)

    lax.fori_loop(0, 2, start_early, 0)
    lax.fori_loop(2, 4, filter_and_start, 0)
    cols_across(0, 128).start()
    cols_over(0, 128).start()
    lax.fori_loop(4, 8, filter_later_rows, 0)

    @pl.when(o > 0)
    def _():
        for copy in halo_copies():
            copy.wait_recv()
        ext[pl.ds(0, 8), :] = halo[...].astype(F32)[8:]

    @pl.when(o == 0)
    def _():
        ext[pl.ds(0, 8), :] = jnp.zeros((8, COLS), F32)
        obs_halo[...] = jnp.zeros((8, 128), F32)

    def first_pieces():
        return [rows_out(m, rel, e, 1 - m) for e in range(2) for m in range(2) for rel in (1, 0)]

    def second_pieces():
        return [rows_out(m, rel, e, m) for e in range(2) for m in range(2) for rel in (1, 0)]

    def passed_on(halves=(0, 1)):
        return [rows_on(m, rel, e) for e in halves for m in range(2) for rel in (1, 0)]

    def arrived(dy, m):
        for rel in (1, 0):
            for e in range(2):
                rows_at(dy, m, rel, e).wait_recv()

    def filter_block(i, _):
        e, m, rel = order(i)
        filter_rows(i, 0)

        @pl.when(e == 0)
        def _():
            rows_out(m, rel, e, 1 - m, 0, 128).start()

        @pl.when(e == 1)
        def _():
            rows_out(m, rel, e, 1 - m).start()

        @pl.when(rel == 1)
        def _():
            rows_over(m, e).start()

        @pl.when(i == 3)
        def _():
            cols_across(0, 0, 128).start()
            cols_over(0, 0, 128).start()

        return 0

    lax.fori_loop(0, 8, filter_block, 0)
    cols_across(1).start()
    cols_over(1).start()
    first_far = near == 2

    @pl.when(first_far)
    def _():
        for copy in second_pieces():
            copy.start()

    def multiply(dy, m, q, e=None):
        role = (near + dy) % 4

        def form():
            at = pl.ds(0, 512)
            value = jnp.dot(rows[dy, m, span(e)], cols[q // 2, q % 2, :, at], preferred_element_type=F32)

            @pl.when(role == 0)
            def _():
                own[m, q, span(e), at] = value

            @pl.when(role != 0)
            def _():
                part[role - 1, m, q, span(e), at] = value.astype(BF16)

        form()

        if q % 2 == 1 and e == 1:
            return
        e = 0 if q % 2 == 1 else e

        @pl.when(role == 2)
        def _():
            x_far(m, q, e).start()

        @pl.when(as_it_is(role, m))
        def _():
            x_raw(role // 2, q, e).start()

    def as_it_is(role, m):
        return jnp.logical_or(jnp.logical_and(role == 1, m == 1), jnp.logical_and(role == 3, m == 0))

    def give(dy, m):
        role = (near + dy) % 4

        @pl.when(role == 0)
        def _():
            giving[m] = own[m, given, span(1)].astype(BF16)
            swap_own(m).start()

        @pl.when(role != 0)
        def _():
            swap(role, m).start()

    def take(dy, m):
        role = (near + dy) % 4

        @pl.when(role == 0)
        def _():
            swap_own(m).wait_recv()
            own[m, kept, span(1)] = own[m, kept, span(1)] + swapped[0, m].astype(F32)

        @pl.when(role != 0)
        def _():
            swap(role, m).wait_recv()
            both = part[role - 1, m, kept, span(1)].astype(F32) + swapped[role, m].astype(F32)
            part[role - 1, m, kept, span(1)] = both.astype(BF16)

        @pl.when(role == 2)
        def _():
            x_far(m, kept, 1, 1).start()

        @pl.when(as_it_is(role, m))
        def _():
            x_raw(role // 2, kept, 1, 1).start()

    def add_far(d, q, valid=True, late=0):
        e = late if late else first_of(q)

        @pl.when(valid)
        def _():
            x_far(d, q, e, late).wait_recv()
            both = part[2 * d, d, q, span(e)].astype(F32) + far[d, q, span(e)].astype(F32)
            part[2 * d, d, q, span(e)] = both.astype(BF16)
            x_sum(d, q, e, late).start()

    def first_of(q):
        return 0 if q % 2 == 1 else None

    def by_near(*values):
        chosen = values[3]
        for place in (2, 1, 0):
            chosen = jnp.where(near == place, values[place], chosen)
        return chosen

    for m in range(2):
        for e in range(2):
            rows_over(m, e).wait_recv()
        cols_over(m).wait_recv()
    for q in range(2):
        for m in (1, 0):
            multiply(0, m, q)

    for e in range(2):
        for m in range(2):
            for rel in (1, 0):
                rows_at(3 - 2 * m, m, rel, e).wait_recv()
        for copy in passed_on((e,)):
            copy.start()
        if e == 1:

            @pl.when(jnp.logical_not(first_far))
            def _():
                for copy in second_pieces():
                    copy.start()

        for q in range(2):
            multiply(3, 0, q, e)
            multiply(1, 1, q, e)
        add_far(by_near(0, 0, 0, 1), e, (near % 2) == 1)
    cols_across(0).wait_recv()
    cols_on(0).start()
    cols_on(0).wait_recv()
    multiply(by_near(3, 0, 0, 0), by_near(0, 1, 1, 1), 2)
    multiply(by_near(1, 0, 0, 0), by_near(1, 0, 0, 0), 2)
    multiply(by_near(0, 3, 3, 3), by_near(1, 0, 0, 0), 2)
    multiply(by_near(0, 1, 1, 1), by_near(0, 1, 1, 1), 2)
    for q in range(2):
        for d in range(2):
            add_far(d, q, near == 2)

    extended = jnp.concatenate([obs_halo[...], signal_row], axis=1)
    total = signal_row
    for lag in range(1, LAGS + 1):
        total = total + taps[lag - 1] * pltpu.roll(extended, lag, 1)[:, 128:]
    small_obs[...] = total[0:1, :].reshape(ROWS)
    obs_out().start()
    weighted[...] = jnp.concatenate([weight_row * total, weight_row * total], axis=0).astype(BF16)
    line = lax.broadcasted_iota(jnp.int32, (8, 128), 0)
    sums = jnp.zeros((8, 128), F32)
    for m in range(2):
        for rel in range(2):
            core = (k + rel) % 2
            dots = lax.dot_general(weighted[...], mine[rel, m], (((1,), (1,)), ((), ())), preferred_element_type=F32)
            for c in range(2):
                sums = jnp.where(line == core * 4 + m * 2 + c, dots[0:8, c * 128 : (c + 1) * 128], sums)
    rhs_all[o] = sums
    for step in range(1, 16):
        rhs_to(step).start()

    third = (by_near(2, 1, 2, 3), by_near(0, 0, 0, 1))
    fourth = (2, by_near(1, 0, 1, 1))
    fifth = (by_near(1, 2, 1, 2), by_near(0, 1, 0, 0))
    sixth = (by_near(3, 3, 3, 1), by_near(1, 1, 1, 0))
    arrived(*third)
    multiply(*third, 2)
    arrived(*fourth)
    multiply(*fourth, 2)
    for q in (0, 1):
        multiply(*third, q)
        multiply(*fourth, q)
    cols_across(1).wait_recv()
    cols_on(1).start()
    cols_on(1).wait_recv()

    def last_sums(q, valid=True):
        add_far(by_near(0, 1, 0, 0), q, valid)
        add_far(1, q, jnp.logical_and(valid, (near % 2) == 0))

    slots = (
        (by_near(2, 1, 0, 3), by_near(0, 0, 1, 1)),
        (by_near(2, 1, 0, 3), by_near(1, 1, 0, 0)),
        (by_near(3, 0, 3, 0), by_near(0, 0, 0, 1)),
        (by_near(1, 0, 1, 0), by_near(1, 1, 1, 0)),
        (by_near(0, 2, 2, 2), by_near(0, 0, 0, 1)),
        (by_near(0, 3, 2, 1), by_near(1, 0, 1, 1)),
    )
    def summed(m, q, e=None, late=0):
        x_sum(m, q, e, late).wait_recv()
        x_raw(1 - m, q, e, late).wait_recv()
        return own[m, q, span(e)] + taken[0, m, q, span(e)].astype(F32) + taken[1, m, q, span(e)].astype(F32)

    def keep_near(c, e=None):
        for m in range(2):
            total = summed(m, c, e)

            @pl.when(settled)
            def _():
                own[m, c, span(e)] = total

            @pl.when(jnp.logical_not(settled))
            def _():
                leaving[0, m, c, span(e)] = total.astype(BF16)
                z_home(m, c, e).start()

    def pass_over(c, e=None):
        for m in (1, 0):
            total = summed(m, 2 + c, e)

            @pl.when(settled)
            def _():
                leaving[1, m, c, span(e)] = total.astype(BF16)
                (z_add(c, e) if m == 0 else z_via(c, e)).start()

            @pl.when(jnp.logical_not(settled))
            def _():
                if m == 0:
                    own[m, 2 + c, span(e)] = total
                else:
                    leaving[1, m, c, span(e)] = total.astype(BF16)
                    z_on(m, c, e).start()

    def hand_on(c, e=None):
        @pl.when(settled)
        def _():
            z_via(c, e).wait_recv()
            z_fwd(c, e).start()

    def add_on(c, e=None):
        @pl.when(jnp.logical_not(settled))
        def _():
            z_add(c, e).wait_recv()
            leaving[1, 0, c, span(e)] = (own[0, 2 + c, span(e)] + landed[1, 0, c, span(e)].astype(F32)).astype(BF16)
            z_on(0, c, e).start()

    def late_sums(valid):
        for d in range(2):
            add_far(d, kept, valid, 1)

    for slot in slots[0:2]:
        multiply(*slot, 3)
        give(*slot)
    add_far(by_near(0, 0, 0, 1), 2, near != 0)
    add_far(1, 2, near == 2)
    for slot in slots[2:6]:
        multiply(*slot, 3)
        give(*slot)
    for piece in (fifth, sixth):
        arrived(*piece)
    for piece in (fifth, sixth):
        multiply(*piece, 2)
    last_sums(2, near != 2)
    for slot in slots[0:2]:
        take(*slot)
    for piece in (fifth, sixth):
        multiply(*piece, 0)
    last_sums(0, near != 2)
    add_far(by_near(0, 0, 0, 1), 3, (near % 2) == 1)
    for piece in (fifth, sixth):
        multiply(*piece, 3)
        multiply(*piece, 1)
        give(*piece)
    for slot in slots[2:4]:
        take(*slot)
    last_sums(3)
    last_sums(1, near == 0)

    @pl.when(near == 0)
    def _():
        pass_over(0)

    for slot in slots[4:6] + (fifth, sixth):
        take(*slot)

    for step in range(1, 16):
        rhs_to(step).wait_recv()
    total = rhs_all[0]
    for step in range(1, 16):
        total = total + rhs_all[step]
    small_rhs[...] = (total * rhs_scale).reshape(COLS)
    rhs_out().start()

    late_sums((near % 2) == 0)
    @pl.when(near != 0)
    def _():
        pass_over(0)

    keep_near(0)
    last_sums(1, (near % 2) == 1)
    late_sums((near % 2) == 1)
    add_on(0)
    pass_over(1, 0)
    hand_on(0)
    keep_near(1, 0)
    add_on(1, 0)
    hand_on(1, 0)
    for m in range(2):
        total = summed(m, kept, 1, 1)

        @pl.when(settled)
        def _():
            own[m, 1, span(1)] = total

        @pl.when(jnp.logical_not(settled))
        def _():
            leaving[1, m, 1, span(1)] = total.astype(BF16)
            z_on(m, 1, 1).start()

    obs_out().wait()
    rhs_out().wait()
    @pl.when(o < 15)
    def _():
        for copy in halo_copies():
            copy.wait_send()

    for m in range(2):
        for e in range(2):
            rows_over(m, e).wait_send()
        cols_over(m).wait_send()
        cols_across(m).wait_send()
        cols_on(m).wait_send()
        swap_own(m).wait_send()
        for role in range(1, 4):
            swap(role, m).wait_send()
        for q in range(4):
            x_far(m, q, first_of(q)).wait_send()
            x_raw(m, q, first_of(q)).wait_send()
            x_sum(m, q, first_of(q)).wait_send()
        x_far(m, kept, 1, 1).wait_send()
        x_raw(m, kept, 1, 1).wait_send()
        x_sum(m, kept, 1, 1).wait_send()
    for copy in first_pieces() + passed_on() + second_pieces():
        copy.wait_send()
    for step in range(1, 16):
        rhs_to(step).wait_send()

    def place(m, c, e, total):
        first, count = m * PART + (128 if e == 1 else 0), PART if e is None else 128
        for b in range(4):
            to = pl.ds(b // 2 * 512 + b % 2 * 256 + c * 128, 128)
            result[pl.ds(first, count), to] = total[:, b * 128 : b * 128 + 128] * scale
        if c == 1:
            leave(m, e).start()

    def leave(m, e):
        half = pl.ds(m * PART + 128 * e, 128)
        return pltpu.make_async_copy(result.at[half], normal.at[half], out_s.at[m, e])

    for c, e in ((0, None), (1, 0), (1, 1)):
        for m in range(2):

            @pl.when(settled)
            def _():
                total = own[m, c, span(e)]
                if e != 1:
                    z_home(m, c, e).wait_recv()
                    total = total + landed[0, m, c, span(e)].astype(F32)
                place(m, c, e, total)

            @pl.when(jnp.logical_not(settled))
            def _():
                z_on(m, c, e).wait_recv()
                total = landed[0, m, c, span(e)].astype(F32)
                if m == 1 and e != 1:
                    z_fwd(c, e).wait_recv()
                    total = total + landed[1, 1, c, span(e)].astype(F32)
                place(m, c, e, total)

    for m in range(2):
        for e in range(2):
            leave(m, e).wait()
    for m in range(2):
        z_on(m, 0).wait_send()
        z_on(m, 1, 0).wait_send()

        @pl.when(settled)
        def _():
            z_fwd(m, first_of(m)).wait_send()

        @pl.when(jnp.logical_not(settled))
        def _():
            z_on(m, 1, 1).wait_send()
            z_home(m, 0).wait_send()
            z_home(m, 1, 0).wait_send()


def per_device(design, observed, row_weight, taps):
    total_rows = ROWS * lax.axis_size("obs")
    dma = pltpu.SemaphoreType.DMA
    vmem = pl.BlockSpec(memory_space=pltpu.VMEM)
    normal, rhs, filtered_obs = pl.pallas_call(
        functools.partial(kernel, 1.0 / total_rows, 1.0 / math.sqrt(total_rows)),
        out_shape=(
            jax.ShapeDtypeStruct((512, COLS), F32),
            jax.ShapeDtypeStruct((COLS,), F32),
            jax.ShapeDtypeStruct((ROWS,), F32),
        ),
        in_specs=[pl.BlockSpec(memory_space=pl.ANY), vmem, vmem, pl.BlockSpec(memory_space=pltpu.SMEM)],
        out_specs=(pl.BlockSpec(memory_space=pl.ANY),) * 3,
        scratch_shapes=[
            pltpu.VMEM((ROWS, COLS), BF16),
            pltpu.VMEM((ROWS + 8, COLS), F32),
            pltpu.VMEM((16, COLS), BF16),
            pltpu.VMEM((8, 128), F32),
            pltpu.VMEM((8, 128), F32),
            pltpu.VMEM((ROWS, 128), F32),
            pltpu.VMEM((2, 2, PART, ROWS), BF16),
            pltpu.VMEM((16, ROWS), BF16),
            pltpu.VMEM((4, 2, PART, DEPTH), BF16),
            pltpu.VMEM((2, 2, DEPTH, 512), BF16),
            pltpu.VMEM((3, 2, 4, PART, 512), BF16),
            pltpu.VMEM((2, 4, PART, 512), F32),
            pltpu.VMEM((2, 2, 4, PART, 512), BF16),
            pltpu.VMEM((2, 4, PART, 512), BF16),
            pltpu.VMEM((2, 128, 512), BF16),
            pltpu.VMEM((4, 2, 128, 512), BF16),
            pltpu.VMEM((2, 2, 2, PART, 512), BF16),
            pltpu.VMEM((2, 2, 2, PART, 512), BF16),
            pltpu.VMEM((2, PART, 512), BF16),
            pltpu.VMEM((512, COLS), F32),
            pltpu.VMEM((ROWS,), F32),
            pltpu.VMEM((COLS,), F32),
            pltpu.VMEM((16, 8, 128), F32),
            dma, dma((2, 2)), dma((2,)), dma((2,)), dma((2,)),
            dma((2, 2, 2, 2)), dma((2, 2, 2)), dma((2, 2)), dma((4, 2, 2, 2)),
            dma((2,)), dma((2,)), dma((2,)), dma((2, 2, 2)),
            dma((2, 6, 4)), dma((2, 6, 4)), dma((4, 2)), dma((4, 2)),
            dma((2, 2, 3)), dma((2, 2, 3)), dma((3,)), dma((3,)),
            dma((16,)), dma((16,)),
        ],
        compiler_params=pltpu.CompilerParams(collective_id=0, has_side_effects=True, vmem_limit_bytes=60 << 20),
        name="normal_equations",
    )(design, observed, row_weight, taps)
    return normal, rhs, filtered_obs


def solution(mesh):
    placed = (P("obs", "param"), P("obs"), P("obs"), P())
    return jax.shard_map(
        per_device,
        mesh=mesh,
        in_specs=placed,
        out_specs=(P("obs", "param"), P("param"), P("obs")),
        check_vma=False,
    )
```

```python
import functools
import math

import jax
import jax.numpy as jnp
from jax import lax
from jax.experimental import pallas as pl
from jax.experimental.pallas import tpu as pltpu
from jax.sharding import PartitionSpec as P

MESH = pl.DeviceIdType.MESH
BF16, F32 = jnp.bfloat16, jnp.float32
ROWS = 640
COLS = 1024
LAGS = 7
PART = 256
DEPTH = 2 * ROWS


def kernel(
    scale, rhs_scale,
    design_hbm, observed, weight, taps,
    normal, rhs, filtered_obs,
    design, ext, halo, obs_tail, obs_halo, wcol, mine, weighted, rows, cols, part, own, taken, far, giving, swapped,
    leaving, landed, passing, result, small_obs, small_rhs, rhs_all,
    design_s, out_s, small_s, halo_s, halo_r, rows_s, rows_f, rows_sib, rows_r, cols_s, cols_sib, cols_f, cols_r, x_s, x_r, swap_s, swap_r, z_s, z_r, z_fs, z_fr, rhs_s, rhs_r,
):
    p, o = lax.axis_index("param"), lax.axis_index("obs")
    y, h = p // 2, p % 2
    x, l, k = o // 4, (o // 2) % 2, o % 2
    near = (y - x + 4) % 4
    settled = l == h
    kept, given = jnp.where(settled, 1, 3), jnp.where(settled, 3, 1)

    def param_of(y_, h_):
        return ((y_ + 4) % 4) * 2 + h_

    def obs_of(x_, l_, k_):
        return ((x_ + 4) % 4) * 4 + l_ * 2 + k_

    sibling = (p, obs_of(x, l, 1 - k))
    across = (param_of(y, 1 - h), o)
    beside = (p, obs_of(x, 1 - l, k))
    corner = (param_of(y, 1 - h), obs_of(x, 1 - l, k))
    following = (p, (o + 1) % 16)

    def remote(src, dst, send, recv, device):
        return pltpu.make_async_remote_copy(
            src_ref=src, dst_ref=dst, send_sem=send, recv_sem=recv, device_id=device, device_id_type=MESH
        )

    def halo_copies():
        return (
            remote(design.at[pl.ds(ROWS - 16, 16), :], halo, halo_s.at[0], halo_r.at[0], following),
            remote(obs_tail, obs_halo, halo_s.at[1], halo_r.at[1], following),
        )

    def lanes(rel):
        return pl.ds(ROWS * rel, ROWS)

    def span(e):
        return pl.ds(0, PART) if e is None else pl.ds(pl.multiple_of(e * 128, 128), 128)

    def wide(c):
        return pl.ds(c * 512, 512)

    def rows_out(m, rel, e, up, begin=0, end=ROWS):
        target = (param_of(y + 2 * up - 1, h), obs_of(x, l, (k + rel) % 2))
        dy = 1 + 2 * up
        to = pl.ds(pl.multiple_of(ROWS * rel + begin, 128), end - begin)
        return remote(
            mine.at[rel, m, span(e), pl.ds(begin, end - begin)], rows.at[dy, m, span(e), to],
            rows_s.at[up, m, rel, e], rows_r.at[dy, m, rel, e], target,
        )

    def rows_on(m, rel, e):
        target = (param_of(y + 1 - 2 * m, h), o)
        return remote(
            rows.at[3 - 2 * m, m, span(e), lanes(rel)], rows.at[2, m, span(e), lanes(rel)],
            rows_f.at[m, rel, e], rows_r.at[2, m, rel, e], target,
        )

    def rows_at(dy, m, rel, e):
        piece = rows.at[dy, m, span(e), lanes(rel)]
        return remote(piece, piece, rows_f.at[0, 0, 0], rows_r.at[dy, m, rel, e], following)

    def rows_over(m, e):
        return remote(mine.at[1, m, span(e)], rows.at[0, m, span(e), lanes(1)], rows_sib.at[m, e], rows_r.at[0, m, 1, e], sibling)

    def cols_over(n, begin=0, end=ROWS):
        half, other = pl.ds(begin, end - begin), pl.ds(ROWS + begin, end - begin)
        return remote(cols.at[0, n, half, :], cols.at[0, n, other, :], cols_sib.at[n], cols_r.at[0, n, 1], sibling)

    def cols_across(n, begin=0, end=ROWS):
        half = pl.ds(begin, end - begin)
        return remote(cols.at[0, n, half, :], cols.at[1, n, half, :], cols_s.at[n], cols_r.at[1, n, 0], across)

    def cols_on(n):
        half = pl.ds(0, ROWS)
        return remote(cols.at[1, n, half, :], cols.at[1, n, pl.ds(ROWS, ROWS), :], cols_f.at[n], cols_r.at[1, n, 1], sibling)

    def beyond(d):
        return (p, obs_of(x + 1 - 2 * d, l, k))

    def x_far(d, q, e=None, late=0):
        at = span(e)
        return remote(part.at[1, d, q, at], far.at[d, q, at], x_s.at[d, 3 * late, q], x_r.at[d, 3 * late, q], beyond(d))

    def x_raw(d, q, e=None, late=0):
        at, kind = span(e), 1 + 3 * late
        dst = taken.at[d, 1 - d, q, at]
        return remote(part.at[2 * d, 1 - d, q, at], dst, x_s.at[d, kind, q], x_r.at[d, kind, q], beyond(d))

    def x_sum(d, q, e=None, late=0):
        at, kind = span(e), 2 + 3 * late
        return remote(part.at[2 * d, d, q, at], taken.at[d, d, q, at], x_s.at[d, kind, q], x_r.at[d, kind, q], beyond(d))

    def swap(role, m):
        place = part.at[role - 1, m, given, span(1)]
        return remote(place, swapped.at[role, m], swap_s.at[role, m], swap_r.at[role, m], beside)

    def swap_own(m):
        return remote(giving.at[m], swapped.at[0, m], swap_s.at[0, m], swap_r.at[0, m], beside)

    def z_home(m, c, e=None):
        sem = step_of(c, e)
        return remote(leaving.at[0, m, c, span(e)], landed.at[0, m, c, span(e)], z_s.at[0, m, sem], z_r.at[0, m, sem], beside)

    def step_of(c, e):
        return c if e is None else c + e

    def z_add(c, e=None):
        sem, at = step_of(c, e), span(e)
        return remote(leaving.at[1, 0, c, at], landed.at[1, 0, c, at], z_s.at[1, 0, sem], z_r.at[1, 0, sem], beside)

    def z_on(m, c, e=None):
        sem, at = step_of(c, e), span(e)
        return remote(leaving.at[1, m, c, at], landed.at[0, m, c, at], z_s.at[1, m, sem], z_r.at[0, m, sem], corner)

    def z_via(c, e=None):
        sem, at = step_of(c, e), span(e)
        return remote(leaving.at[1, 1, c, at], passing.at[c, at], z_s.at[1, 1, sem], z_r.at[1, 1, sem], corner)

    def z_fwd(c, e=None):
        sem, at = step_of(c, e), span(e)
        return remote(passing.at[c, at], landed.at[1, 1, c, at], z_fs.at[sem], z_fr.at[sem], beside)

    def obs_out():
        return pltpu.make_async_copy(small_obs, filtered_obs, small_s.at[0])

    def rhs_out():
        return pltpu.make_async_copy(small_rhs, rhs, small_s.at[1])

    def rhs_to(step):
        peer = (p, (o + step) % 16)
        return remote(rhs_all.at[o], rhs_all.at[o], rhs_s.at[step], rhs_r.at[step], peer)

    incoming = pltpu.make_async_copy(design_hbm, design, design_s)
    incoming.start()

    barrier = pltpu.get_barrier_semaphore()
    greeted = [(param_of(y + step, h), obs_of(x, l, core)) for step in (1, -1) for core in (k, 1 - k)] + [across, corner]
    greeted += [(p, (o + step) % 16) for step in range(1, 16)]
    for device in greeted:
        pl.semaphore_signal(barrier, inc=1, device_id=device, device_id_type=MESH)

    signal_row = jnp.broadcast_to(observed[...].astype(F32).reshape(1, ROWS), (8, ROWS))
    weight_row = jnp.broadcast_to(weight[...].reshape(1, ROWS), (8, ROWS))
    obs_tail[...] = signal_row[:, ROWS - 128 :]
    for r in range(ROWS // 128):
        block = jnp.broadcast_to(weight_row[0:1, r * 128 : (r + 1) * 128], (128, 128))
        wcol[pl.ds(r * 128, 128), :] = block.T

    def order(i):
        return i // 4, i % 2, 1 - (i // 2) % 2

    def filter_rows(i, r):
        e, m, rel = order(i)
        core = (k + rel) % 2
        at = pl.ds(pl.multiple_of(core * 512 + m * PART + e * 128, 128), 128)
        quarter = pl.ds(pl.multiple_of((core * 2 + m) * 128, 128), 128)
        first = r * 128
        total = ext[pl.ds(8 + first, 128), at]
        for lag in range(1, LAGS + 1):
            total = total + taps[lag - 1] * ext[pl.ds(8 + first - lag, 128), at]
        rounded = total.astype(BF16).astype(F32)
        cols[0, e, pl.ds(first, 128), quarter] = (wcol[pl.ds(first, 128), :] * rounded).astype(BF16)
        turned = rounded.T.astype(BF16)
        mine[rel, m, span(e), pl.ds(first, 128)] = turned

        @pl.when(rel == 0)
        def _():
            rows[0, m, span(e), pl.ds(first, 128)] = turned

    def filter_later_rows(i, _):
        e, m, rel = order(i)
        at = pl.ds(pl.multiple_of((k + rel) % 2 * 512 + m * PART + e * 128, 128), 128)
        ext[pl.ds(8, ROWS), at] = design[:, at].astype(F32)
        for r in range(1, ROWS // 128):
            filter_rows(i, r)
        return 0

    incoming.wait()
    lax.fori_loop(0, 2, filter_later_rows, 0)
    pl.semaphore_wait(barrier, len(greeted))

    @pl.when(o < 15)
    def _():
        for copy in halo_copies():
            copy.start()

    def start_early(i, _):
        e, m, rel = order(i)
        rows_out(m, rel, 0, 1 - m, 128).start()
        return 0

    def filter_and_start(i, _):
        filter_later_rows(i, _)
        return start_early(i, _)

    lax.fori_loop(0, 2, start_early, 0)
    lax.fori_loop(2, 4, filter_and_start, 0)
    cols_across(0, 128).start()
    cols_over(0, 128).start()
    lax.fori_loop(4, 8, filter_later_rows, 0)

    @pl.when(o > 0)
    def _():
        for copy in halo_copies():
            copy.wait_recv()
        ext[pl.ds(0, 8), :] = halo[...].astype(F32)[8:]

    @pl.when(o == 0)
    def _():
        ext[pl.ds(0, 8), :] = jnp.zeros((8, COLS), F32)
        obs_halo[...] = jnp.zeros((8, 128), F32)

    def first_pieces():
        return [rows_out(m, rel, e, 1 - m) for e in range(2) for m in range(2) for rel in (1, 0)]

    def second_pieces():
        return [rows_out(m, rel, e, m) for e in range(2) for m in range(2) for rel in (1, 0)]

    def passed_on(halves=(0, 1)):
        return [rows_on(m, rel, e) for e in halves for m in range(2) for rel in (1, 0)]

    def arrived(dy, m):
        for rel in (1, 0):
            for e in range(2):
                rows_at(dy, m, rel, e).wait_recv()

    def filter_block(i, _):
        e, m, rel = order(i)
        filter_rows(i, 0)

        @pl.when(e == 0)
        def _():
            rows_out(m, rel, e, 1 - m, 0, 128).start()

        @pl.when(e == 1)
        def _():
            rows_out(m, rel, e, 1 - m).start()

        @pl.when(rel == 1)
        def _():
            rows_over(m, e).start()

        @pl.when(i == 3)
        def _():
            cols_across(0, 0, 128).start()
            cols_over(0, 0, 128).start()

        return 0

    lax.fori_loop(0, 8, filter_block, 0)
    cols_across(1).start()
    cols_over(1).start()
    first_far = near == 2

    @pl.when(first_far)
    def _():
        for copy in second_pieces():
            copy.start()

    def multiply(dy, m, q, e=None):
        role = (near + dy) % 4

        def form():
            at = pl.ds(0, 512)
            value = jnp.dot(rows[dy, m, span(e)], cols[q // 2, q % 2, :, at], preferred_element_type=F32)

            @pl.when(role == 0)
            def _():
                own[m, q, span(e), at] = value

            @pl.when(role != 0)
            def _():
                part[role - 1, m, q, span(e), at] = value.astype(BF16)

        form()

        if q % 2 == 1 and e == 1:
            return
        e = 0 if q % 2 == 1 else e

        @pl.when(role == 2)
        def _():
            x_far(m, q, e).start()

        @pl.when(as_it_is(role, m))
        def _():
            x_raw(role // 2, q, e).start()

    def as_it_is(role, m):
        return jnp.logical_or(jnp.logical_and(role == 1, m == 1), jnp.logical_and(role == 3, m == 0))

    def give(dy, m):
        role = (near + dy) % 4

        @pl.when(role == 0)
        def _():
            giving[m] = own[m, given, span(1)].astype(BF16)
            swap_own(m).start()

        @pl.when(role != 0)
        def _():
            swap(role, m).start()

    def take(dy, m):
        role = (near + dy) % 4

        @pl.when(role == 0)
        def _():
            swap_own(m).wait_recv()
            own[m, kept, span(1)] = own[m, kept, span(1)] + swapped[0, m].astype(F32)

        @pl.when(role != 0)
        def _():
            swap(role, m).wait_recv()
            both = part[role - 1, m, kept, span(1)].astype(F32) + swapped[role, m].astype(F32)
            part[role - 1, m, kept, span(1)] = both.astype(BF16)

        @pl.when(role == 2)
        def _():
            x_far(m, kept, 1, 1).start()

        @pl.when(as_it_is(role, m))
        def _():
            x_raw(role // 2, kept, 1, 1).start()

    def add_far(d, q, valid=True, late=0):
        e = late if late else first_of(q)

        @pl.when(valid)
        def _():
            x_far(d, q, e, late).wait_recv()
            both = part[2 * d, d, q, span(e)].astype(F32) + far[d, q, span(e)].astype(F32)
            part[2 * d, d, q, span(e)] = both.astype(BF16)
            x_sum(d, q, e, late).start()

    def first_of(q):
        return 0 if q % 2 == 1 else None

    def by_near(*values):
        chosen = values[3]
        for place in (2, 1, 0):
            chosen = jnp.where(near == place, values[place], chosen)
        return chosen

    for m in range(2):
        for e in range(2):
            rows_over(m, e).wait_recv()
        cols_over(m).wait_recv()
    for q in range(2):
        for m in (1, 0):
            multiply(0, m, q)

    for e in range(2):
        for m in range(2):
            for rel in (1, 0):
                rows_at(3 - 2 * m, m, rel, e).wait_recv()
        for copy in passed_on((e,)):
            copy.start()
        if e == 1:

            @pl.when(jnp.logical_not(first_far))
            def _():
                for copy in second_pieces():
                    copy.start()

        for q in range(2):
            multiply(3, 0, q, e)
            multiply(1, 1, q, e)
        add_far(by_near(0, 0, 0, 1), e, (near % 2) == 1)
    cols_across(0).wait_recv()
    cols_on(0).start()
    cols_on(0).wait_recv()
    multiply(by_near(3, 0, 0, 0), by_near(0, 1, 1, 1), 2)
    multiply(by_near(1, 0, 0, 0), by_near(1, 0, 0, 0), 2)
    multiply(by_near(0, 3, 3, 3), by_near(1, 0, 0, 0), 2)
    multiply(by_near(0, 1, 1, 1), by_near(0, 1, 1, 1), 2)
    for q in range(2):
        for d in range(2):
            add_far(d, q, near == 2)

    extended = jnp.concatenate([obs_halo[...], signal_row], axis=1)
    total = signal_row
    for lag in range(1, LAGS + 1):
        total = total + taps[lag - 1] * pltpu.roll(extended, lag, 1)[:, 128:]
    small_obs[...] = total[0:1, :].reshape(ROWS)
    obs_out().start()
    weighted[...] = jnp.concatenate([weight_row * total, weight_row * total], axis=0).astype(BF16)
    line = lax.broadcasted_iota(jnp.int32, (8, 128), 0)
    sums = jnp.zeros((8, 128), F32)
    for m in range(2):
        for rel in range(2):
            core = (k + rel) % 2
            dots = lax.dot_general(weighted[...], mine[rel, m], (((1,), (1,)), ((), ())), preferred_element_type=F32)
            for c in range(2):
                sums = jnp.where(line == core * 4 + m * 2 + c, dots[0:8, c * 128 : (c + 1) * 128], sums)
    rhs_all[o] = sums
    for step in range(1, 16):
        rhs_to(step).start()

    third = (by_near(2, 1, 2, 3), by_near(0, 0, 0, 1))
    fourth = (2, by_near(1, 0, 1, 1))
    fifth = (by_near(1, 2, 1, 2), by_near(0, 1, 0, 0))
    sixth = (by_near(3, 3, 3, 1), by_near(1, 1, 1, 0))
    arrived(*third)
    multiply(*third, 2)
    arrived(*fourth)
    multiply(*fourth, 2)
    for q in (0, 1):
        multiply(*third, q)
        multiply(*fourth, q)
    cols_across(1).wait_recv()
    cols_on(1).start()
    cols_on(1).wait_recv()

    def last_sums(q, valid=True):
        add_far(by_near(0, 1, 0, 0), q, valid)
        add_far(1, q, jnp.logical_and(valid, (near % 2) == 0))

    slots = (
        (by_near(2, 1, 0, 3), by_near(0, 0, 1, 1)),
        (by_near(2, 1, 0, 3), by_near(1, 1, 0, 0)),
        (by_near(3, 0, 3, 0), by_near(0, 0, 0, 1)),
        (by_near(1, 0, 1, 0), by_near(1, 1, 1, 0)),
        (by_near(0, 2, 2, 2), by_near(0, 0, 0, 1)),
        (by_near(0, 3, 2, 1), by_near(1, 0, 1, 1)),
    )
    def summed(m, q, e=None, late=0):
        x_sum(m, q, e, late).wait_recv()
        x_raw(1 - m, q, e, late).wait_recv()
        return own[m, q, span(e)] + taken[0, m, q, span(e)].astype(F32) + taken[1, m, q, span(e)].astype(F32)

    def keep_near(c, e=None):
        for m in range(2):
            total = summed(m, c, e)

            @pl.when(settled)
            def _():
                own[m, c, span(e)] = total

            @pl.when(jnp.logical_not(settled))
            def _():
                leaving[0, m, c, span(e)] = total.astype(BF16)
                z_home(m, c, e).start()

    def pass_over(c, e=None):
        for m in (1, 0):
            total = summed(m, 2 + c, e)

            @pl.when(settled)
            def _():
                leaving[1, m, c, span(e)] = total.astype(BF16)
                (z_add(c, e) if m == 0 else z_via(c, e)).start()

            @pl.when(jnp.logical_not(settled))
            def _():
                if m == 0:
                    own[m, 2 + c, span(e)] = total
                else:
                    leaving[1, m, c, span(e)] = total.astype(BF16)
                    z_on(m, c, e).start()

    def hand_on(c, e=None):
        @pl.when(settled)
        def _():
            z_via(c, e).wait_recv()
            z_fwd(c, e).start()

    def add_on(c, e=None):
        @pl.when(jnp.logical_not(settled))
        def _():
            z_add(c, e).wait_recv()
            leaving[1, 0, c, span(e)] = (own[0, 2 + c, span(e)] + landed[1, 0, c, span(e)].astype(F32)).astype(BF16)
            z_on(0, c, e).start()

    def late_sums(valid):
        for d in range(2):
            add_far(d, kept, valid, 1)

    for slot in slots[0:2]:
        multiply(*slot, 3)
        give(*slot)
    add_far(by_near(0, 0, 0, 1), 2, near != 0)
    add_far(1, 2, near == 2)
    for slot in slots[2:6]:
        multiply(*slot, 3)
        give(*slot)
    for piece in (fifth, sixth):
        arrived(*piece)
    for piece in (fifth, sixth):
        multiply(*piece, 2)
    last_sums(2, near != 2)
    for slot in slots[0:2]:
        take(*slot)
    for piece in (fifth, sixth):
        multiply(*piece, 0)
    last_sums(0, near != 2)
    add_far(by_near(0, 0, 0, 1), 3, (near % 2) == 1)
    for piece in (fifth, sixth):
        multiply(*piece, 3)
        multiply(*piece, 1)
        give(*piece)
    for slot in slots[2:4]:
        take(*slot)
    last_sums(3)
    last_sums(1, near == 0)

    @pl.when(near == 0)
    def _():
        pass_over(0)

    for slot in slots[4:6] + (fifth, sixth):
        take(*slot)

    for step in range(1, 16):
        rhs_to(step).wait_recv()
    total = rhs_all[0]
    for step in range(1, 16):
        total = total + rhs_all[step]
    small_rhs[...] = (total * rhs_scale).reshape(COLS)
    rhs_out().start()

    late_sums((near % 2) == 0)
    @pl.when(near != 0)
    def _():
        pass_over(0)

    last_sums(1, (near % 2) == 1)
    late_sums((near % 2) == 1)
    keep_near(0)
    add_on(0)
    pass_over(1, 0)
    hand_on(0)
    keep_near(1, 0)
    add_on(1, 0)
    hand_on(1, 0)
    for m in range(2):
        total = summed(m, kept, 1, 1)

        @pl.when(settled)
        def _():
            own[m, 1, span(1)] = total

        @pl.when(jnp.logical_not(settled))
        def _():
            leaving[1, m, 1, span(1)] = total.astype(BF16)
            z_on(m, 1, 1).start()

    obs_out().wait()
    rhs_out().wait()
    @pl.when(o < 15)
    def _():
        for copy in halo_copies():
            copy.wait_send()

    for m in range(2):
        for e in range(2):
            rows_over(m, e).wait_send()
        cols_over(m).wait_send()
        cols_across(m).wait_send()
        cols_on(m).wait_send()
        swap_own(m).wait_send()
        for role in range(1, 4):
            swap(role, m).wait_send()
        for q in range(4):
            x_far(m, q, first_of(q)).wait_send()
            x_raw(m, q, first_of(q)).wait_send()
            x_sum(m, q, first_of(q)).wait_send()
        x_far(m, kept, 1, 1).wait_send()
        x_raw(m, kept, 1, 1).wait_send()
        x_sum(m, kept, 1, 1).wait_send()
    for copy in first_pieces() + passed_on() + second_pieces():
        copy.wait_send()
    for step in range(1, 16):
        rhs_to(step).wait_send()

    def place(m, c, e, total):
        first, count = m * PART + (128 if e == 1 else 0), PART if e is None else 128
        for b in range(4):
            to = pl.ds(b // 2 * 512 + b % 2 * 256 + c * 128, 128)
            result[pl.ds(first, count), to] = total[:, b * 128 : b * 128 + 128] * scale
        if c == 1:
            leave(m, e).start()

    def leave(m, e):
        half = pl.ds(m * PART + 128 * e, 128)
        return pltpu.make_async_copy(result.at[half], normal.at[half], out_s.at[m, e])

    for c, e in ((0, None), (1, 0), (1, 1)):
        for m in range(2):

            @pl.when(settled)
            def _():
                total = own[m, c, span(e)]
                if e != 1:
                    z_home(m, c, e).wait_recv()
                    total = total + landed[0, m, c, span(e)].astype(F32)
                place(m, c, e, total)

            @pl.when(jnp.logical_not(settled))
            def _():
                z_on(m, c, e).wait_recv()
                total = landed[0, m, c, span(e)].astype(F32)
                if m == 1 and e != 1:
                    z_fwd(c, e).wait_recv()
                    total = total + landed[1, 1, c, span(e)].astype(F32)
                place(m, c, e, total)

    for m in range(2):
        for e in range(2):
            leave(m, e).wait()
    for m in range(2):
        z_on(m, 0).wait_send()
        z_on(m, 1, 0).wait_send()

        @pl.when(settled)
        def _():
            z_fwd(m, first_of(m)).wait_send()

        @pl.when(jnp.logical_not(settled))
        def _():
            z_on(m, 1, 1).wait_send()
            z_home(m, 0).wait_send()
            z_home(m, 1, 0).wait_send()


def per_device(design, observed, row_weight, taps):
    total_rows = ROWS * lax.axis_size("obs")
    dma = pltpu.SemaphoreType.DMA
    vmem = pl.BlockSpec(memory_space=pltpu.VMEM)
    normal, rhs, filtered_obs = pl.pallas_call(
        functools.partial(kernel, 1.0 / total_rows, 1.0 / math.sqrt(total_rows)),
        out_shape=(
            jax.ShapeDtypeStruct((512, COLS), F32),
            jax.ShapeDtypeStruct((COLS,), F32),
            jax.ShapeDtypeStruct((ROWS,), F32),
        ),
        in_specs=[pl.BlockSpec(memory_space=pl.ANY), vmem, vmem, pl.BlockSpec(memory_space=pltpu.SMEM)],
        out_specs=(pl.BlockSpec(memory_space=pl.ANY),) * 3,
        scratch_shapes=[
            pltpu.VMEM((ROWS, COLS), BF16),
            pltpu.VMEM((ROWS + 8, COLS), F32),
            pltpu.VMEM((16, COLS), BF16),
            pltpu.VMEM((8, 128), F32),
            pltpu.VMEM((8, 128), F32),
            pltpu.VMEM((ROWS, 128), F32),
            pltpu.VMEM((2, 2, PART, ROWS), BF16),
            pltpu.VMEM((16, ROWS), BF16),
            pltpu.VMEM((4, 2, PART, DEPTH), BF16),
            pltpu.VMEM((2, 2, DEPTH, 512), BF16),
            pltpu.VMEM((3, 2, 4, PART, 512), BF16),
            pltpu.VMEM((2, 4, PART, 512), F32),
            pltpu.VMEM((2, 2, 4, PART, 512), BF16),
            pltpu.VMEM((2, 4, PART, 512), BF16),
            pltpu.VMEM((2, 128, 512), BF16),
            pltpu.VMEM((4, 2, 128, 512), BF16),
            pltpu.VMEM((2, 2, 2, PART, 512), BF16),
            pltpu.VMEM((2, 2, 2, PART, 512), BF16),
            pltpu.VMEM((2, PART, 512), BF16),
            pltpu.VMEM((512, COLS), F32),
            pltpu.VMEM((ROWS,), F32),
            pltpu.VMEM((COLS,), F32),
            pltpu.VMEM((16, 8, 128), F32),
            dma, dma((2, 2)), dma((2,)), dma((2,)), dma((2,)),
            dma((2, 2, 2, 2)), dma((2, 2, 2)), dma((2, 2)), dma((4, 2, 2, 2)),
            dma((2,)), dma((2,)), dma((2,)), dma((2, 2, 2)),
            dma((2, 6, 4)), dma((2, 6, 4)), dma((4, 2)), dma((4, 2)),
            dma((2, 2, 3)), dma((2, 2, 3)), dma((3,)), dma((3,)),
            dma((16,)), dma((16,)),
        ],
        compiler_params=pltpu.CompilerParams(collective_id=0, has_side_effects=True, vmem_limit_bytes=60 << 20),
        name="normal_equations",
    )(design, observed, row_weight, taps)
    return normal, rhs, filtered_obs


def solution(mesh):
    placed = (P("obs", "param"), P("obs"), P("obs"), P())
    return jax.shard_map(
        per_device,
        mesh=mesh,
        in_specs=placed,
        out_specs=(P("obs", "param"), P("param"), P("obs")),
        check_vma=False,
    )
```
